256 devices in a mesh: orb: 4 (over z_hi, core), space: 64 (over z_lo, y, x).
Axes of the slice: x: 4, y: 4, z: 8 (z_hi: 2, z_lo: 4; z = z_hi * 4 + z_lo), core: 2. Of those that a mesh axis runs over, the one named last changes fastest.
Arguments:
- orbitals: float32 [4, 384, 64, 256], P('orb', 'space'), may hold values from -80 to 80
- atom_type: int32 [384, 64, 256], P('space'), may hold values from 0 to 7
- type_table: float32 [8], replicated, may hold values from -6 to 2
- step_length: float32 [4], replicated, may hold values from 0.1 to 0.4
Outputs:
- new_orbitals: float32 [4, 384, 64, 256], P('orb', 'space')
The draws below stay inside these ranges and needn't reach their ends.
All inputs are finite; a program needn't handle non-finite values.
Results may differ from the reference program's by a relative error of at most 0.00035.
Values sent between devices are 32-bit elements; how exact they have to be, the bound alone decides.
A program may use at most 128 MiB of HBM per device.

```python
import math
import jax
import jax.numpy as jnp
from jax import lax

NY = 64
NZ = 256
NTYPES = 8
NORB = 4
NX = 384


def draw_orbitals(key, part):
    key = jax.random.fold_in(key, 11)
    first_key = jax.random.fold_in(key, 1)
    second_key = jax.random.fold_in(key, 2)
    phase_key = jax.random.fold_in(key, 3)
    plane_x = jnp.arange(NX, dtype=jnp.float32)
    plane_y = jnp.arange(NY, dtype=jnp.int32)
    plane_z = jnp.arange(NZ, dtype=jnp.float32)
    rise_x = jnp.sqrt(1.0 + 2.0 * plane_x / (NX - 1))
    spread_y = jnp.exp(0.5 * math.log(10.0) * (plane_y * 37 % NY).astype(jnp.float32) / NY)
    envelope = rise_x[:, None, None] * spread_y[None, :, None]
    phases = jax.random.uniform(phase_key, (3,), jnp.float32, 0.0, 2.0 * math.pi)
    amplitude = 1.0 + 0.5 * jax.random.uniform(jax.random.fold_in(phase_key, 1), (), jnp.float32)
    wave_x = jnp.sin(math.pi * (plane_x + 0.5) / NX)
    wave_y = 1.0 + 0.5 * jnp.cos(2.0 * math.pi * plane_y.astype(jnp.float32) / NY + phases[0])
    wave_z = 1.0 + 0.5 * jnp.cos(2.0 * math.pi * plane_z / NZ + phases[1])
    gentle = amplitude * wave_x[:, None, None] * wave_y[None, :, None] * wave_z[None, None, :]
    index = jnp.arange(NORB, dtype=jnp.int32)
    denom = max(NORB - 1, 1)
    gentle_weight = 0.4 + 1.2 * (index * 5 % NORB).astype(jnp.float32) / denom
    rough_weight = 0.4 + 0.5 * ((index + 2) % NORB).astype(jnp.float32) / denom
    common = jnp.clip(jax.random.normal(first_key, (NX, NY, NZ), jnp.float32), -4.0, 4.0)
    single = jnp.clip(jax.random.normal(second_key, (NORB, NX, NY, NZ), jnp.float32), -4.0, 4.0)
    field = gentle_weight[:, None, None, None] * gentle[None] + rough_weight[:, None, None, None] * common[None] + single
    return (field * envelope[None]).astype(jnp.float32)


def touch_ends(result, own_key, low, top_value):
    dims = result.shape
    index_at = [jax.random.randint(jax.random.fold_in(own_key, axis), (), 0, dims[axis]) for axis in range(len(dims))]
    result = result.at[tuple(index_at)].set(low)
    longest = dims.index(max(dims))
    index_at[longest] = (index_at[longest] + 1) % dims[longest]
    return result.at[tuple(index_at)].set(top_value)


def setup_inputs(seed: int = 0) -> dict:
    arg_keys = jax.random.split(jax.random.key(seed), 5)
    orbitals = draw_orbitals(jax.random.fold_in(arg_keys[4], 71), 0)
    atom_type = touch_ends(jax.random.randint(arg_keys[1], (NX, NY, NZ), 0, NTYPES), jax.random.fold_in(arg_keys[1], 1), 0, NTYPES - 1).astype(jnp.int32)
    type_table = jnp.clip(jax.random.uniform(arg_keys[2], (NTYPES,), jnp.float32, -6.0, 2.0), -6.0, 2.0)
    step_length = jnp.clip(jnp.exp(jax.random.uniform(arg_keys[3], (NORB,), jnp.float32, math.log(0.1), math.log(0.4))), 0.1, 0.4)
    return {"orbitals": orbitals, "atom_type": atom_type, "type_table": type_table, "step_length": step_length}


CENTER_TAP = -5369.0 / 1800.0
SIDE_TAPS = (12.0 / 7.0, -15.0 / 56.0, 10.0 / 189.0, -1.0 / 112.0, 2.0 / 1925.0, -1.0 / 16632.0)
SHIFT = 1.0
DAMPING = 0.6
DIAGONAL = SHIFT - 1.5 * CENTER_TAP
HIGH = lax.Precision.HIGHEST

def laplacian(field):
    width = field.shape[1]
    padded = jnp.pad(field, ((0, 0), (6, 6), (0, 0), (0, 0)))
    total = 3.0 * CENTER_TAP * field
    for offset, weight in enumerate(SIDE_TAPS, 1):
        near = padded[:, 6 + offset:6 + offset + width] + padded[:, 6 - offset:6 - offset + width]
        near = near + jnp.roll(field, offset, 2) + jnp.roll(field, -offset, 2)
        near = near + jnp.roll(field, offset, 3) + jnp.roll(field, -offset, 3)
        total = total + weight * near
    return total

def smooth(gradient):
    search = DAMPING * gradient / DIAGONAL
    for sweep in range(2):
        search = search + DAMPING * (gradient + 0.5 * laplacian(search) - SHIFT * search) / DIAGONAL
    return search

def reference(orbitals, atom_type, type_table, step_length):
    potential = jnp.zeros(atom_type.shape, jnp.float32)
    for kind in range(NTYPES):
        potential = potential + jnp.where(atom_type == kind, type_table[kind], jnp.float32(0.0))
    applied = -0.5 * laplacian(orbitals) + potential[None] * orbitals
    count = orbitals.shape[1] * orbitals.shape[2] * orbitals.shape[3]
    flat = orbitals.reshape(NORB, -1)
    margin = jnp.dot(flat, flat.T, precision=HIGH) / count
    projected = jnp.dot(flat, applied.reshape(NORB, -1).T, precision=HIGH) / count
    factor = jnp.linalg.cholesky(margin)
    coupling = jax.scipy.linalg.cho_solve((factor, True), projected)
    gradient = applied - jnp.dot(coupling.T, flat, precision=HIGH).reshape(orbitals.shape)
    search = smooth(gradient)
    moved = orbitals - step_length[:, None, None, None] * search
    moved_flat = moved.reshape(NORB, -1)
    metric = jnp.dot(moved_flat, moved_flat.T, precision=HIGH) / count
    lower = jnp.linalg.cholesky(metric)
    inverse = jax.scipy.linalg.solve_triangular(lower, jnp.eye(NORB, dtype=jnp.float32), lower=True)
    rotation = inverse.T
    return jnp.dot(rotation.T, moved_flat, precision=HIGH).reshape(orbitals.shape)
```

```python
import jax
import jax.numpy as jnp
import numpy as np
from jax import lax
from jax.experimental import pallas as pl
from jax.experimental.pallas import tpu as pltpu
from jax.sharding import PartitionSpec as P

MESH = pl.DeviceIdType.MESH
HIGH = lax.Precision.HIGHEST
CENTER_TAP = -5369.0 / 1800.0
SIDE_TAPS = (12.0 / 7.0, -15.0 / 56.0, 10.0 / 189.0, -1.0 / 112.0, 2.0 / 1925.0, -1.0 / 16632.0)
SHIFT = 1.0
DAMPING = 0.6
DIAGONAL = SHIFT - 1.5 * CENTER_TAP
CELLS = 384 * 64 * 256
NORB = 4
NTYPES = 8

SIDE = tuple(-0.5 * w for w in SIDE_TAPS)
CENTER = -1.5 * CENTER_TAP
W = DAMPING / DIAGONAL
P1, P2, P3 = 3.0 * W, -3.0 * W * W, W * W * W

PL, RW, CO = 12, 16, 128
H = 6
PAIRS = [(i, j) for i in range(NORB) for j in range(i + 1)]


def z_tables():
    own = np.zeros((CO, CO), np.float32)
    for a in range(CO):
        for b in range(CO):
            d = abs(a - b)
            if d == 0:
                own[a, b] = CENTER
            elif d <= H:
                own[a, b] = SIDE[d - 1]
    pick = np.zeros((16, CO), np.float32)
    spread = np.zeros((16, CO), np.float32)
    for i in range(H):
        pick[i, CO - H + i] = 1.0
        pick[H + i, i] = 1.0
        for b in range(CO):
            d = b + H - i
            if 1 <= d <= H:
                spread[i, b] = SIDE[d - 1]
            d = CO + i - b
            if 1 <= d <= H:
                spread[H + i, b] = SIDE[d - 1]
    return own, pick, spread


def dot(a, b, ca, cb):
    return lax.dot_general(
        a, b, (((ca,), (cb,)), ((), ())), precision=HIGH, preferred_element_type=jnp.float32
    )


def cholesky(s):
    low = {}
    inv = []
    for i in range(NORB):
        for j in range(i):
            t = s[i, j]
            for k in range(j):
                t = t - low[i, k] * low[j, k]
            low[i, j] = t * inv[j]
        t = s[i, i]
        for k in range(i):
            t = t - low[i, k] * low[i, k]
        root = jnp.sqrt(t)
        low[i, i] = root
        inv.append(1.0 / root)
    return low, inv


def kernel(
    x_ref, type_ref, own_ref, pick_ref, spread_ref, table_ref, step_ref, out_ref,
    xf, wf, gf, vs, vf, mx, mw, base, new, zz, zs, zr, gram, coef, ra, rb,
    t_send, t_recv, v_send, v_recv, h_send, h_recv, b_send, b_recv, r_send, r_recv,
):
    s = lax.axis_index("space")
    o = lax.axis_index("orb")
    h, c, q, x = o // 2, o % 2, s // 4, s % 4
    mine = c == x // 2
    link = 2 * q + c
    has_left, has_right = link > 0, link < 31

    def device(hh, cc, qq, xx):
        return (2 * hh + cc, 4 * qq + xx)

    left = device(h, (link + 31) % 2, ((link + 31) % 32) // 2, x)
    right = device(h, (link + 1) % 2, ((link + 1) % 32) // 2, x)
    up = device(h, c, q, (x + 3) % 4)
    down = device(h, c, q, (x + 1) % 4)
    across = device(1 - h, c, q, x)

    me1 = (x * 2 + h) * 2 + c
    me2 = q

    def peer1(k):
        i = (me1 + k) % 16
        return device((i // 2) % 2, i % 2, q, i // 4)

    def peer2(k):
        return device(h, c, (me2 + k) % 16, x)

    barrier = pltpu.get_barrier_semaphore()

    def hello(k, carry):
        pl.semaphore_signal(barrier, inc=1, device_id=peer1(k), device_id_type=MESH)
        pl.semaphore_signal(barrier, inc=1, device_id=peer2(k), device_id_type=MESH)
        return carry

    lax.fori_loop(1, 16, hello, 0)

    @pl.when(jnp.logical_and(c == 0, has_left))
    def _():
        pl.semaphore_signal(barrier, inc=1, device_id=left, device_id_type=MESH)

    @pl.when(jnp.logical_and(c == 1, has_right))
    def _():
        pl.semaphore_signal(barrier, inc=1, device_id=right, device_id_type=MESH)

    kinds = type_ref[...]
    potential = jnp.zeros(kinds.shape, jnp.float32)
    for kind in range(NTYPES):
        potential = jnp.where(kinds == kind, table_ref[kind], potential)
    vs[...] = potential

    for f in (xf, wf, gf):
        @pl.when(jnp.logical_not(has_left))
        def _():
            f[:, 0:H] = jnp.zeros((NORB, H, RW + 16, CO), jnp.float32)

        @pl.when(jnp.logical_not(has_right))
        def _():
            f[:, H + PL:] = jnp.zeros((NORB, H, RW + 16, CO), jnp.float32)
    gram[...] = jnp.zeros(gram.shape, jnp.float32)

    @pl.when(jnp.logical_or(jnp.logical_and(c == 0, has_left), jnp.logical_and(c == 1, has_right)))
    def _():
        pl.semaphore_wait(barrier, 31)

    @pl.when(jnp.logical_not(jnp.logical_or(jnp.logical_and(c == 0, has_left), jnp.logical_and(c == 1, has_right))))
    def _():
        pl.semaphore_wait(barrier, 30)

    def rows_of(xx):
        return pl.ds(pl.multiple_of(16 * xx, 16), 16)

    def cols_of(hh):
        return pl.ds(pl.multiple_of(CO * hh, CO), CO)

    def part(ref, xx, hh):
        return ref.at[:, rows_of(xx), cols_of(hh)]

    half = x % 2

    def scatter(j, k):
        hh, xx = (h + j) % 2, (x + k) % 4
        n = 4 * j + k
        return part(x_ref, xx, hh), xf.at[o, pl.ds(H + 6 * half, 6), pl.ds(8, 16)], t_send.at[n], t_recv.at[2 * o + half], device(hh, x // 2, q, xx)

    def remote(src, dst, ss, rs, dev):
        return pltpu.make_async_remote_copy(
            src_ref=src, dst_ref=dst, send_sem=ss, recv_sem=rs, device_id=dev, device_id_type=MESH
        )

    for j in (1, 0):
        for k in (2, 1, 3, 0):
            a = scatter(j, k)
            if j == 0 and k == 0:
                @pl.when(mine)
                def _():
                    pltpu.make_async_copy(a[0], a[1], a[3]).start()

                @pl.when(jnp.logical_not(mine))
                def _():
                    remote(*a).start()
            else:
                remote(*a).start()

    def spread_v(k, n):
        xx = (x + k) % 4
        return part(vs, xx, h), vf.at[pl.ds(6 * half, 6)], v_send.at[n], v_recv.at[half], device(h, x // 2, q, xx)

    @pl.when(mine)
    def _():
        a = spread_v(0, 0)
        pltpu.make_async_copy(a[0], a[1], a[3]).start()
        remote(*spread_v(2, 1)).start()

    @pl.when(jnp.logical_not(mine))
    def _():
        remote(*spread_v(1, 0)).start()
        remote(*spread_v(3, 1)).start()

    own = (slice(H, H + PL), slice(8, 8 + RW))

    def halo_copies(f, r):
        full = slice(None)
        return (
            (has_left, remote(f.at[:, H:2 * H, 8:8 + RW], f.at[:, H + PL:, 8:8 + RW], h_send.at[5 * r], h_recv.at[5 * r + 1], left)),
            (has_right, remote(f.at[:, PL:PL + H, 8:8 + RW], f.at[:, 0:H, 8:8 + RW], h_send.at[5 * r + 1], h_recv.at[5 * r], right)),
            (None, remote(f.at[:, H:H + PL, 8:16], f.at[:, H:H + PL, 24:32], h_send.at[5 * r + 2], h_recv.at[5 * r + 3], up)),
            (None, remote(f.at[:, H:H + PL, 16:24], f.at[:, H:H + PL, 0:8], h_send.at[5 * r + 3], h_recv.at[5 * r + 2], down)),
            (None, remote(zs.at[r], zr.at[r], h_send.at[5 * r + 4], h_recv.at[5 * r + 4], across)),
        )

    def guarded(cond, fn):
        if cond is None:
            fn()
        else:
            pl.when(cond)(fn)

    def share(f):
        return f[:, own[0], own[1]].reshape(NORB * PL * RW, CO)

    def halo_start(f, r):
        copies = halo_copies(f, r)
        flat = share(f)
        zs[r] = dot(pick_ref[...], flat, 1, 1)
        for cond, cp in (copies[4],) + copies[:4]:
            guarded(cond, cp.start)
        zz[...] = dot(flat, own_ref[...], 1, 0)

    def halo_finish(f, r):
        copies = halo_copies(f, r)
        for cond, cp in copies:
            guarded(cond, cp.wait_send)
        guarded(has_left, copies[1][1].wait_recv)
        guarded(has_right, copies[0][1].wait_recv)
        for _, cp in copies[2:]:
            cp.wait_recv()
        zz[...] += dot(zr[r], spread_ref[...], 0, 0)

    def kinetic(f, i, p):
        at = pl.ds(pl.multiple_of((i * PL + p) * RW, RW), RW)
        total = zz[at]
        for n in range(1, H + 1):
            near = f[i, p + H + n, 8:8 + RW] + f[i, p + H - n, 8:8 + RW]
            near = near + f[i, p + H, 8 + n:8 + RW + n] + f[i, p + H, 8 - n:8 + RW - n]
            total = total + SIDE[n - 1] * near
        return total

    def each(fn):
        def step(n, carry):
            fn(n // PL, n % PL)
            return carry
        lax.fori_loop(0, NORB * PL, step, 0)

    def each_plane(fn):
        def step(p, carry):
            fn(p)
            return carry
        lax.fori_loop(0, PL, step, 0)

    def reduce_start(v, buf, send, recv, me, peer):
        buf[me] = v

        def go(k, carry):
            remote(buf.at[me], buf.at[me], send, recv, peer(k)).start()
            return carry

        lax.fori_loop(1, 16, go, 0)

    def reduce_finish(buf, send, recv, peer):
        cp = remote(buf.at[pl.ds(0, 15)], buf.at[pl.ds(0, 15)], send, recv, peer(1))
        cp.wait_send()
        cp.wait_recv()
        return jnp.sum(buf[...], axis=0)

    def local_sums(rows):
        for n, v in enumerate(rows):
            gram[n:n + 1] = jnp.sum(v, axis=0, keepdims=True)
        return dot(jnp.ones((8, CO), jnp.float32), gram[...], 1, 1)[0:1]

    def spread_out(v, n):
        return jnp.broadcast_to(v[:, n:n + 1], (8, CO)) * (1.0 / CELLS)

    def planes(f, i, p, halo=True):
        v = f[i, p + H, 8:8 + RW] if halo else f[i, p]
        return v.reshape(2, 8, CO)

    for i in range(NORB):
        for p in range(2):
            cp = remote(xf.at[i, pl.ds(H + 6 * p, 6), pl.ds(8, 16)], xf.at[i, pl.ds(H + 6 * p, 6), pl.ds(8, 16)], t_send.at[0], t_recv.at[2 * i + p], across)
            cp.wait_recv()
    halo_start(xf, 0)
    for p in range(2):
        remote(vf.at[pl.ds(6 * p, 6)], vf.at[pl.ds(6 * p, 6)], v_send.at[0], v_recv.at[p], across).wait_recv()
    halo_finish(xf, 0)

    def first(i, p):
        kx = kinetic(xf, i, p)
        v = xf[i, p + H, 8:8 + RW]
        wf[i, p + H, 8:8 + RW] = kx + vf[p] * v
        mx[i, p] = kx + SHIFT * v

    each(first)
    halo_start(wf, 1)

    def products(p, acc):
        xs = [planes(xf, i, p) for i in range(NORB)]
        ws = [planes(wf, i, p) for i in range(NORB)]
        acc = list(acc)
        for n, (i, j) in enumerate(PAIRS):
            acc[n] = acc[n] + jnp.sum(xs[i] * xs[j], axis=0)
        for j in range(NORB):
            for i in range(NORB):
                n = 10 + 4 * j + i
                acc[n] = acc[n] + jnp.sum(xs[j] * ws[i], axis=0)
        return tuple(acc)

    zero = jnp.zeros((8, CO), jnp.float32)
    acc = lax.fori_loop(0, PL, products, (zero,) * 26)
    reduce_start(local_sums(acc), ra.at[0], r_send.at[0], r_recv.at[0], me1, peer1)
    v = reduce_finish(ra.at[0], r_send.at[0], r_recv.at[0], peer1)
    reduce_start(v, rb.at[0], r_send.at[1], r_recv.at[1], me2, peer2)
    halo_finish(wf, 1)

    def second(i, p):
        mw[i, p] = kinetic(wf, i, p) + SHIFT * wf[i, p + H, 8:8 + RW]

    each(second)
    v = reduce_finish(rb.at[0], r_send.at[1], r_recv.at[1], peer2)
    margin = {(i, j): spread_out(v, n) for n, (i, j) in enumerate(PAIRS)}
    low, inv = cholesky(margin)
    for i in range(NORB):
        y = []
        for j in range(NORB):
            t = spread_out(v, 10 + 4 * j + i)
            for k in range(j):
                t = t - low[j, k] * y[k]
            y.append(t * inv[j])
        for j in reversed(range(NORB)):
            t = y[j]
            for k in range(j + 1, NORB):
                t = t - low[k, j] * y[k]
            y[j] = t * inv[j]
            coef[4 * i + j] = y[j]

    def couple(p):
        ms = [planes(mx, j, p, False) for j in range(NORB)]
        for i in range(NORB):
            t = planes(mw, i, p, False)
            for j in range(NORB):
                t = t - coef[4 * i + j] * ms[j]
            gf[i, p + H, 8:8 + RW] = t.reshape(RW, CO)

    each_plane(couple)
    halo_start(gf, 2)

    def prepare(p):
        xs = [planes(xf, j, p) for j in range(NORB)]
        for i in range(NORB):
            t = planes(wf, i, p)
            for j in range(NORB):
                t = t - coef[4 * i + j] * xs[j]
            t = P1 * t + (P2 + SHIFT * P3) * planes(gf, i, p)
            base[i, p] = (xs[i] - step_ref[i] * t).reshape(RW, CO)

    each_plane(prepare)
    halo_finish(gf, 2)

    def third(i, p):
        base[i, p] = base[i, p] - (P3 * step_ref[i]) * kinetic(gf, i, p)

    each(third)

    def metric(p, acc):
        ms = [planes(base, i, p, False) for i in range(NORB)]
        return tuple(a + jnp.sum(ms[i] * ms[j], axis=0) for a, (i, j) in zip(acc, PAIRS))

    acc = lax.fori_loop(0, PL, metric, (zero,) * 10)
    reduce_start(local_sums(acc), ra.at[1], r_send.at[2], r_recv.at[2], me1, peer1)
    v = reduce_finish(ra.at[1], r_send.at[2], r_recv.at[2], peer1)
    reduce_start(v, rb.at[1], r_send.at[3], r_recv.at[3], me2, peer2)
    v = reduce_finish(rb.at[1], r_send.at[3], r_recv.at[3], peer2)
    low, inv = cholesky({(i, j): spread_out(v, n) for n, (i, j) in enumerate(PAIRS)})
    lowinv = {}
    for j in range(NORB):
        lowinv[j, j] = inv[j]
        for i in range(j + 1, NORB):
            t = low[i, j] * lowinv[j, j]
            for k in range(j + 1, i):
                t = t + low[i, k] * lowinv[k, j]
            lowinv[i, j] = -t * inv[i]
    for n, ij in enumerate(PAIRS):
        coef[n] = lowinv[ij]

    def rotate(p):
        ms = [planes(base, j, p, False) for j in range(NORB)]
        for i in range(NORB):
            t = None
            for n, (a, j) in enumerate(PAIRS):
                if a == i:
                    term = coef[n] * ms[j]
                    t = term if t is None else t + term
            new[i, p] = t.reshape(RW, CO)

    each_plane(rotate)

    def back(j, i, m):
        hh, cc, pp = (h + j) % 2, (c + i) % 2, (x + m) % 2
        return new.at[2 * hh + cc, pl.ds(6 * pp, 6)], part(out_ref, x, h), b_send.at[4 * j + 2 * i + m], b_recv.at[2 * x + h], device(hh, cc, q, 2 * c + pp)

    order = [(j, i, m) for j in (1, 0) for i in (1, 0) for m in (1, 0)]
    for jim in order:
        a = back(*jim)
        if jim == (0, 0, 0):
            @pl.when(mine)
            def _():
                pltpu.make_async_copy(a[0], a[1], a[3]).start()

            @pl.when(jnp.logical_not(mine))
            def _():
                remote(*a).start()
        else:
            remote(*a).start()

    for j in (1, 0):
        for k in (2, 1, 3, 0):
            a = scatter(j, k)
            if j == 0 and k == 0:
                @pl.when(jnp.logical_not(mine))
                def _():
                    remote(*a).wait_send()
            else:
                remote(*a).wait_send()

    @pl.when(mine)
    def _():
        remote(*spread_v(2, 1)).wait_send()

    @pl.when(jnp.logical_not(mine))
    def _():
        remote(*spread_v(1, 0)).wait_send()
        remote(*spread_v(3, 1)).wait_send()

    for jim in order:
        a = back(*jim)
        if jim == (0, 0, 0):
            @pl.when(jnp.logical_not(mine))
            def _():
                remote(*a).wait_send()
        else:
            remote(*a).wait_send()
    for xx in range(4):
        for hh in range(2):
            dst = out_ref.at[:, pl.ds(16 * xx, 16), pl.ds(CO * hh, CO)]
            remote(dst, dst, b_send.at[0], b_recv.at[2 * xx + hh], across).wait_recv()


def body(orbitals, atom_type, type_table, step_length):
    shape = orbitals.shape
    own, pick, spread = z_tables()
    vmem = pl.BlockSpec(memory_space=pltpu.VMEM)
    smem = pl.BlockSpec(memory_space=pltpu.SMEM)
    f32 = jnp.float32
    share = (NORB, PL, RW, CO)
    wide = (NORB, PL + 2 * H, RW + 16, CO)
    rows = NORB * PL * RW
    dma = pltpu.SemaphoreType.DMA
    out = pl.pallas_call(
        kernel,
        out_shape=jax.ShapeDtypeStruct(shape[1:], f32),
        in_specs=[vmem] * 5 + [smem] * 2,
        out_specs=vmem,
        scratch_shapes=[
            pltpu.VMEM(wide, f32), pltpu.VMEM(wide, f32), pltpu.VMEM(wide, f32),
            pltpu.VMEM(shape[1:], f32), pltpu.VMEM((PL, RW, CO), f32),
            pltpu.VMEM(share, f32), pltpu.VMEM(share, f32), pltpu.VMEM(share, f32), pltpu.VMEM(share, f32),
            pltpu.VMEM((rows, CO), f32),
            pltpu.VMEM((3, 16, rows), f32), pltpu.VMEM((3, 16, rows), f32),
            pltpu.VMEM((CO, CO), f32), pltpu.VMEM((16, 8, CO), f32),
            pltpu.VMEM((2, 16, 1, CO), f32), pltpu.VMEM((2, 16, 1, CO), f32),
            dma((8,)), dma((8,)), dma((2,)), dma((2,)), dma((15,)), dma((15,)),
            dma((8,)), dma((8,)), dma((4,)), dma((4,)),
        ],
        compiler_params=pltpu.CompilerParams(
            collective_id=0, has_side_effects=True, vmem_limit_bytes=40 << 20
        ),
        name="step",
    )(orbitals.reshape(shape[1:]), atom_type, own, pick, spread, type_table, step_length)
    return out.reshape(shape)


def solution(mesh):
    in_specs = (P("orb", "space", None, None), P("space", None, None), P(), P())
    out_specs = P("orb", "space", None, None)
    return jax.shard_map(body, mesh=mesh, in_specs=in_specs, out_specs=out_specs, check_vma=False)
```

```python
import jax
import jax.numpy as jnp
from jax import lax
from jax.experimental import pallas as pl
from jax.experimental.pallas import tpu as pltpu
from jax.sharding import PartitionSpec as P

MESH = pl.DeviceIdType.MESH
HIGH = lax.Precision.HIGHEST
CENTER_TAP = -5369.0 / 1800.0
SIDE_TAPS = (12.0 / 7.0, -15.0 / 56.0, 10.0 / 189.0, -1.0 / 112.0, 2.0 / 1925.0, -1.0 / 16632.0)
SHIFT = 1.0
DAMPING = 0.6
DIAGONAL = SHIFT - 1.5 * CENTER_TAP
CELLS = 384 * 64 * 256
NORB = 4
NTYPES = 8

SIDE = tuple(-0.5 * w for w in SIDE_TAPS)
CENTER = -1.5 * CENTER_TAP
W = DAMPING / DIAGONAL
P1, P2, P3 = 3.0 * W, -3.0 * W * W, W * W * W

PL, RW, CO = 12, 16, 128
H = 6
PAIRS = [(i, j) for i in range(NORB) for j in range(i + 1)]


def iota(shape, dim):
    return lax.broadcasted_iota(jnp.int32, shape, dim)


def taps_at(distance, centre):
    out = jnp.zeros(distance.shape, jnp.float32)
    if centre is not None:
        out = jnp.where(distance == 0, jnp.float32(centre), out)
    for n, w in enumerate(SIDE, 1):
        out = jnp.where(distance == n, jnp.float32(w), out)
    return out


def dot(a, b, ca, cb):
    return lax.dot_general(
        a, b, (((ca,), (cb,)), ((), ())), precision=HIGH, preferred_element_type=jnp.float32
    )


def cholesky(s):
    low = {}
    inv = []
    for i in range(NORB):
        for j in range(i):
            t = s[i, j]
            for k in range(j):
                t = t - low[i, k] * low[j, k]
            low[i, j] = t * inv[j]
        t = s[i, i]
        for k in range(i):
            t = t - low[i, k] * low[i, k]
        root = jnp.sqrt(t)
        low[i, i] = root
        inv.append(1.0 / root)
    return low, inv


def kernel(
    x_hbm, type_hbm, table_hbm, step_hbm, out_ref,
    x_ref, type_ref, table_ref, step_ref, own_ref, pick_ref, spread_ref,
    xf, wf, nf, mf, vs, vf, base, vv, new, zz, zd_out, zd, zs, zr, gram, coef, ra, rb,
    in_sem, t_send, t_recv, d_send, d_recv, v_send, v_recv, h_send, h_recv, b_send, b_recv, r_send, r_recv,
):
    s = lax.axis_index("space")
    o = lax.axis_index("orb")
    h, c, q, x = o // 2, o % 2, s // 4, s % 4
    side = (c + q) % 2
    host = (x // 2 + q) % 2
    mine = c == host
    link = 2 * q + side
    has_left, has_right = link > 0, link < 31

    def device(hh, cc, qq, xx):
        return (2 * hh + cc, 4 * qq + xx)

    def along(n):
        n = n % 32
        return device(h, (n + n // 2) % 2, n // 2, x)

    left, right = along(link + 31), along(link + 1)
    up = device(h, c, q, (x + 3) % 4)
    down = device(h, c, q, (x + 1) % 4)
    across = device(1 - h, c, q, x)

    me1 = (x * 2 + h) * 2 + c
    me2 = q

    def peer1(k):
        i = (me1 + k) % 16
        return device((i // 2) % 2, i % 2, q, i // 4)

    def peer2(k):
        return device(h, c, (me2 + k) % 16, x)

    loads = [
        pltpu.make_async_copy(src, dst, in_sem.at[n])
        for n, (src, dst) in enumerate(
            ((x_hbm, x_ref), (type_hbm, type_ref), (table_hbm, table_ref), (step_hbm, step_ref))
        )
    ]
    for cp in loads:
        cp.start()

    barrier = pltpu.get_barrier_semaphore()

    def hello(k, carry):
        pl.semaphore_signal(barrier, inc=1, device_id=peer1(k), device_id_type=MESH)
        pl.semaphore_signal(barrier, inc=1, device_id=peer2(k), device_id_type=MESH)
        return carry

    lax.fori_loop(1, 16, hello, 0)

    own_ref[...] = taps_at(jnp.abs(iota((CO, CO), 0) - iota((CO, CO), 1)), CENTER)
    row, col = iota((16, CO), 0), iota((16, CO), 1)
    target = jnp.where(row < H, CO - H + row, jnp.where(row < 2 * H, row - H, -1))
    pick_ref[...] = jnp.where(col == target, jnp.float32(1.0), jnp.float32(0.0))
    spread_ref[...] = taps_at(
        jnp.where(row < H, col + H - row, jnp.where(row < 2 * H, CO + row - H - col, 0)), None
    )
    gram[...] = jnp.zeros(gram.shape, jnp.float32)
    for f in (xf, wf, nf, mf):
        @pl.when(jnp.logical_not(has_left))
        def _():
            f[:, 0:H] = jnp.zeros((NORB, H, RW + 16, CO), jnp.float32)

        @pl.when(jnp.logical_not(has_right))
        def _():
            f[:, H + PL:] = jnp.zeros((NORB, H, RW + 16, CO), jnp.float32)

    def rows_of(xx):
        return pl.ds(pl.multiple_of(16 * xx, 16), 16)

    def cols_of(hh):
        return pl.ds(pl.multiple_of(CO * hh, CO), CO)

    def part(ref, xx, hh):
        return ref.at[:, rows_of(xx), cols_of(hh)]

    def remote(src, dst, ss, rs, dev):
        return pltpu.make_async_remote_copy(
            src_ref=src, dst_ref=dst, send_sem=ss, recv_sem=rs, device_id=dev, device_id_type=MESH
        )

    def guarded(cond, fn):
        if cond is None:
            fn()
        else:
            pl.when(cond)(fn)

    loads[0].wait()
    for k in range(4):
        edge = x_ref[:, rows_of((x + k) % 4), cols_of(1 - h)].reshape(6 * RW, CO)
        zd_out[k, :, 0:6 * RW] = dot(pick_ref[...], edge, 1, 1)

    for cp in loads[1:]:
        cp.wait()
    kinds = type_ref[...]
    potential = jnp.zeros(kinds.shape, jnp.float32)
    for kind in range(NTYPES):
        potential = jnp.where(kinds == kind, table_ref[kind], potential)
    vs[...] = potential

    pl.semaphore_wait(barrier, 30)

    half = x % 2

    def scatter(j, k):
        hh, xx = (h + j) % 2, (x + k) % 4
        n = 4 * j + k
        return part(x_ref, xx, hh), xf.at[o, pl.ds(H + 6 * half, 6), pl.ds(8, 16)], t_send.at[n], t_recv.at[2 * o + half], device(hh, host, q, xx)

    def edges(k):
        return zd_out.at[k], zd.at[c, half], d_send.at[k], d_recv.at[2 * c + half], device(h, host, q, (x + k) % 4)

    def potentials(k, n):
        xx = (x + k) % 4
        return part(vs, xx, h), vf.at[pl.ds(6 * half, 6)], v_send.at[n], v_recv.at[half], device(h, host, q, xx)

    def local_or_remote(a):
        @pl.when(mine)
        def _():
            pltpu.make_async_copy(a[0], a[1], a[3]).start()

        @pl.when(jnp.logical_not(mine))
        def _():
            remote(*a).start()

    for k in (2, 1, 3, 0):
        remote(*scatter(1, k)).start()
    for k in (2, 1, 3, 0):
        if k == 0:
            local_or_remote(scatter(0, 0))
            local_or_remote(edges(0))
        else:
            remote(*scatter(0, k)).start()
            remote(*edges(k)).start()

    @pl.when(mine)
    def _():
        a = potentials(0, 0)
        pltpu.make_async_copy(a[0], a[1], a[3]).start()
        remote(*potentials(2, 1)).start()

    @pl.when(jnp.logical_not(mine))
    def _():
        remote(*potentials(1, 0)).start()
        remote(*potentials(3, 1)).start()

    A, B = h, 1 - h

    def halo_copies(f, r, pair):
        at = pl.ds(2 * pair, 2)
        m = 10 * r + 5 * pair
        return (
            (has_left, remote(f.at[at, H:2 * H, 8:8 + RW], f.at[at, H + PL:, 8:8 + RW], h_send.at[m], h_recv.at[m + 1], left)),
            (has_right, remote(f.at[at, PL:PL + H, 8:8 + RW], f.at[at, 0:H, 8:8 + RW], h_send.at[m + 1], h_recv.at[m], right)),
            (None, remote(f.at[at, H:H + PL, 8:14], f.at[at, H:H + PL, 24:30], h_send.at[m + 2], h_recv.at[m + 3], up)),
            (None, remote(f.at[at, H:H + PL, 18:24], f.at[at, H:H + PL, 2:8], h_send.at[m + 3], h_recv.at[m + 2], down)),
            (None, remote(zs.at[r, pair], zr.at[r, pair], h_send.at[m + 4], h_recv.at[m + 4], across)),
        )

    def share(f, pair):
        return f[pl.ds(2 * pair, 2), H:H + PL, 8:8 + RW].reshape(2 * PL * RW, CO)

    def halo_start(f, r, pair, with_z=True):
        copies = halo_copies(f, r, pair)
        flat = share(f, pair)
        if with_z:
            zs[r, pair] = dot(pick_ref[...], flat, 1, 1)
            copies[4][1].start()
        for n in (0, 1, 2, 3):
            guarded(copies[n][0], copies[n][1].start)
        zz[r, pair] = dot(flat, own_ref[...], 1, 0)

    def halo_finish(f, r, pair, with_z=True):
        copies = halo_copies(f, r, pair)
        guarded(has_left, copies[1][1].wait_recv)
        guarded(has_right, copies[0][1].wait_recv)
        copies[2][1].wait_recv()
        copies[3][1].wait_recv()
        if with_z:
            copies[4][1].wait_recv()
            zz[r, pair] += dot(zr[r, pair], spread_ref[...], 0, 0)

    def halo_sent(f, r, pair, with_z=True):
        for cond, cp in halo_copies(f, r, pair)[:5 if with_z else 4]:
            guarded(cond, cp.wait_send)

    def kinetic(f, r, pair, i, p):
        total = zz[r, pair, pl.ds(pl.multiple_of((i * PL + p) * RW, RW), RW)]
        i = 2 * pair + i
        for n in range(1, H + 1):
            near = f[i, p + H + n, 8:8 + RW] + f[i, p + H - n, 8:8 + RW]
            near = near + f[i, p + H, 8 + n:8 + RW + n] + f[i, p + H, 8 - n:8 + RW - n]
            total = total + SIDE[n - 1] * near
        return total

    def each(fn, pair):
        def step(n, carry):
            fn(pair, n // PL, n % PL)
            return carry
        lax.fori_loop(0, 2 * PL, step, 0, unroll=4)

    def each_plane(fn, init=0):
        return lax.fori_loop(0, PL, fn, init, unroll=2)

    def reduce_start(v, buf, send, recv, me, peer):
        buf[me] = v

        def go(k, carry):
            remote(buf.at[me], buf.at[me], send, recv, peer(k)).start()
            return carry

        lax.fori_loop(1, 16, go, 0)

    def reduce_finish(buf, send, recv, peer):
        cp = remote(buf.at[pl.ds(0, 15)], buf.at[pl.ds(0, 15)], send, recv, peer(1))
        cp.wait_send()
        cp.wait_recv()
        return jnp.sum(buf[...], axis=0)

    def local_sums(rows):
        for n, v in enumerate(rows):
            gram[n:n + 1] = jnp.sum(v, axis=0, keepdims=True)
        return dot(jnp.ones((8, CO), jnp.float32), gram[...], 1, 1)[0:1]

    def spread_out(v, n):
        return jnp.broadcast_to(v[:, n:n + 1], (8, CO)) * (1.0 / CELLS)

    def wide(f, i, p):
        return f[i, p + H, 8:8 + RW].reshape(2, 8, CO)

    def narrow(f, i, p):
        return f[i, p].reshape(2, 8, CO)

    def first(pair, i, p):
        k = kinetic(xf, 0, pair, i, p)
        i = 2 * pair + i
        v = xf[i, p + H, 8:8 + RW]
        wf[i, p + H, 8:8 + RW] = k + vf[p] * v
        nf[i, p + H, 8:8 + RW] = k + SHIFT * v

    def second(pair, i, p):
        k = kinetic(wf, 1, pair, i, p)
        i = 2 * pair + i
        mf[i, p + H, 8:8 + RW] = k + SHIFT * wf[i, p + H, 8:8 + RW]

    def smooth_x(pair, i, p):
        k = kinetic(nf, 2, pair, i, p)
        i = 2 * pair + i
        vv[i, p] = P1 * xf[i, p + H, 8:8 + RW] + (P2 + SHIFT * P3) * nf[i, p + H, 8:8 + RW] + P3 * k

    def smooth_w(pair, i, p):
        k = kinetic(mf, 3, pair, i, p)
        i = 2 * pair + i
        t = P1 * wf[i, p + H, 8:8 + RW] + (P2 + SHIFT * P3) * mf[i, p + H, 8:8 + RW] + P3 * k
        base[i, p] = xf[i, p + H, 8:8 + RW] - step_ref[i] * t

    def arrived(pair):
        for i in range(2):
            for p in range(2):
                ref = xf.at[2 * pair + i, pl.ds(H + 6 * p, 6), pl.ds(8, 16)]
                remote(ref, ref, t_send.at[0], t_recv.at[2 * (2 * pair + i) + p], across).wait_recv()

    arrived(A)
    halo_start(xf, 0, A)
    arrived(B)
    halo_start(xf, 0, B, False)
    for i in range(2):
        for p in range(2):
            remote(zd.at[i, p], zd.at[i, p], d_send.at[0], d_recv.at[2 * i + p], across).wait_recv()
            at = pl.ds((2 * i + p) * 6 * RW, 6 * RW)
            zz[0, A, at] += dot(zd[i, p][:, 0:6 * RW], spread_ref[...], 0, 0)
    for p in range(2):
        remote(vf.at[pl.ds(6 * p, 6)], vf.at[pl.ds(6 * p, 6)], v_send.at[0], v_recv.at[p], across).wait_recv()
    halo_finish(xf, 0, A, False)
    each(first, A)
    halo_start(wf, 1, A)
    halo_finish(xf, 0, B)
    each(first, B)
    halo_start(wf, 1, B)
    halo_start(nf, 2, A)
    halo_start(nf, 2, B)

    def products(p, acc):
        xs = [wide(xf, i, p) for i in range(NORB)]
        ws = [wide(wf, i, p) for i in range(NORB)]
        acc = list(acc)
        for n, (i, j) in enumerate(PAIRS):
            acc[n] = acc[n] + jnp.sum(xs[i] * xs[j], axis=0)
        for j in range(NORB):
            for i in range(NORB):
                n = 10 + 4 * j + i
                acc[n] = acc[n] + jnp.sum(xs[j] * ws[i], axis=0)
        return tuple(acc)

    zero = jnp.zeros((8, CO), jnp.float32)
    acc = each_plane(products, (zero,) * 26)
    reduce_start(local_sums(acc), ra.at[0], r_send.at[0], r_recv.at[0], me1, peer1)

    halo_finish(wf, 1, A)
    each(second, A)
    halo_start(mf, 3, A)
    halo_finish(wf, 1, B)
    each(second, B)
    halo_start(mf, 3, B)
    halo_finish(nf, 2, A)
    each(smooth_x, A)
    v = reduce_finish(ra.at[0], r_send.at[0], r_recv.at[0], peer1)
    reduce_start(v, rb.at[0], r_send.at[1], r_recv.at[1], me2, peer2)
    halo_finish(nf, 2, B)
    each(smooth_x, B)
    halo_finish(mf, 3, A)
    each(smooth_w, A)
    halo_finish(mf, 3, B)
    each(smooth_w, B)

    v = reduce_finish(rb.at[0], r_send.at[1], r_recv.at[1], peer2)
    margin = {(i, j): spread_out(v, n) for n, (i, j) in enumerate(PAIRS)}
    low, inv = cholesky(margin)
    for i in range(NORB):
        y = []
        for j in range(NORB):
            t = spread_out(v, 10 + 4 * j + i)
            for k in range(j):
                t = t - low[j, k] * y[k]
            y.append(t * inv[j])
        for j in reversed(range(NORB)):
            t = y[j]
            for k in range(j + 1, NORB):
                t = t - low[k, j] * y[k]
            y[j] = t * inv[j]
            coef[4 * i + j] = step_ref[i] * y[j]

    def move(p, acc):
        vs4 = [narrow(vv, j, p) for j in range(NORB)]
        ms = []
        for i in range(NORB):
            t = narrow(base, i, p)
            for j in range(NORB):
                t = t + coef[4 * i + j] * vs4[j]
            base[i, p] = t.reshape(RW, CO)
            ms.append(t)
        return tuple(a + jnp.sum(ms[i] * ms[j], axis=0) for a, (i, j) in zip(acc, PAIRS))

    acc = each_plane(move, (zero,) * 10)
    reduce_start(local_sums(acc), ra.at[1], r_send.at[2], r_recv.at[2], me1, peer1)
    v = reduce_finish(ra.at[1], r_send.at[2], r_recv.at[2], peer1)
    reduce_start(v, rb.at[1], r_send.at[3], r_recv.at[3], me2, peer2)
    v = reduce_finish(rb.at[1], r_send.at[3], r_recv.at[3], peer2)
    low, inv = cholesky({(i, j): spread_out(v, n) for n, (i, j) in enumerate(PAIRS)})
    lowinv = {}
    for j in range(NORB):
        lowinv[j, j] = inv[j]
        for i in range(j + 1, NORB):
            t = low[i, j] * lowinv[j, j]
            for k in range(j + 1, i):
                t = t + low[i, k] * lowinv[k, j]
            lowinv[i, j] = -t * inv[i]
    for n, ij in enumerate(PAIRS):
        coef[n] = lowinv[ij]

    def rotate(p, carry):
        ms = [narrow(base, j, p) for j in range(NORB)]
        for i in range(NORB):
            t = None
            for n, (a, j) in enumerate(PAIRS):
                if a == i:
                    term = coef[n] * ms[j]
                    t = term if t is None else t + term
            new[i, p] = t.reshape(RW, CO)
        return carry

    each_plane(rotate)

    def back(j, i, m):
        hh, cc, pp = (h + j) % 2, (c + i) % 2, (x + m) % 2
        return new.at[2 * hh + cc, pl.ds(6 * pp, 6)], part(out_ref, x, h), b_send.at[4 * j + 2 * i + m], b_recv.at[2 * x + h], device(hh, cc, q, 2 * side + pp)

    order = [(j, i, m) for j in (1, 0) for i in (1, 0) for m in (1, 0)]
    for jim in order:
        a = back(*jim)
        if jim == (0, 0, 0):
            local_or_remote(a)
        else:
            remote(*a).start()

    unless_mine = jnp.logical_not(mine)
    for k in range(4):
        remote(*scatter(1, k)).wait_send()
        guarded(unless_mine if k == 0 else None, remote(*scatter(0, k)).wait_send)
        guarded(unless_mine if k == 0 else None, remote(*edges(k)).wait_send)

    @pl.when(mine)
    def _():
        remote(*potentials(2, 1)).wait_send()

    @pl.when(unless_mine)
    def _():
        remote(*potentials(1, 0)).wait_send()
        remote(*potentials(3, 1)).wait_send()

    for r, f in enumerate((xf, wf, nf, mf)):
        halo_sent(f, r, A)
        halo_sent(f, r, B, r > 0)
    for jim in order:
        guarded(unless_mine if jim == (0, 0, 0) else None, remote(*back(*jim)).wait_send)
    for xx in range(4):
        for hh in range(2):
            dst = out_ref.at[:, pl.ds(16 * xx, 16), pl.ds(CO * hh, CO)]
            remote(dst, dst, b_send.at[0], b_recv.at[2 * xx + hh], across).wait_recv()


def body(orbitals, atom_type, type_table, step_length):
    shape = orbitals.shape
    slab = shape[1:]
    anywhere = pl.BlockSpec(memory_space=pl.ANY)
    f32 = jnp.float32
    share = (NORB, PL, RW, CO)
    wide = (NORB, PL + 2 * H, RW + 16, CO)
    rows = 2 * PL * RW
    dma = pltpu.SemaphoreType.DMA

    def vmem(*shape):
        return pltpu.VMEM(shape, f32)

    out = pl.pallas_call(
        kernel,
        out_shape=jax.ShapeDtypeStruct(slab, f32),
        in_specs=[anywhere] * 4,
        out_specs=pl.BlockSpec(memory_space=pltpu.VMEM),
        scratch_shapes=[
            vmem(*slab), pltpu.VMEM(slab, jnp.int32), pltpu.SMEM((NTYPES,), f32), pltpu.SMEM((NORB,), f32),
            vmem(CO, CO), vmem(16, CO), vmem(16, CO),
            vmem(*wide), vmem(*wide), vmem(*wide), vmem(*wide),
            vmem(*slab), vmem(PL, RW, CO), vmem(*share), vmem(*share), vmem(*share),
            vmem(4, 2, rows, CO), vmem(4, 16, CO), vmem(2, 2, 16, CO),
            vmem(4, 2, 16, rows), vmem(4, 2, 16, rows),
            vmem(CO, CO), vmem(16, 8, CO), vmem(2, 16, 1, CO), vmem(2, 16, 1, CO),
            dma((4,)), dma((8,)), dma((8,)), dma((4,)), dma((4,)), dma((2,)), dma((2,)),
            dma((40,)), dma((40,)), dma((8,)), dma((8,)), dma((4,)), dma((4,)),
        ],
        compiler_params=pltpu.CompilerParams(
            collective_id=0, has_side_effects=True, vmem_limit_bytes=55993958
        ),
        name="step",
    )(orbitals.reshape(slab), atom_type, type_table, step_length)
    return out.reshape(shape)


def solution(mesh):
    in_specs = (P("orb", "space", None, None), P("space", None, None), P(), P())
    out_specs = P("orb", "space", None, None)
    return jax.shard_map(body, mesh=mesh, in_specs=in_specs, out_specs=out_specs, check_vma=False)
```

```python
import functools

import jax
import jax.numpy as jnp
from jax import lax
from jax.experimental import pallas as pl
from jax.experimental.pallas import tpu as pltpu
from jax.sharding import PartitionSpec as P

MESH = pl.DeviceIdType.MESH
HIGH = lax.Precision.HIGHEST
CENTER_TAP = -5369.0 / 1800.0
SIDE_TAPS = (12.0 / 7.0, -15.0 / 56.0, 10.0 / 189.0, -1.0 / 112.0, 2.0 / 1925.0, -1.0 / 16632.0)
SHIFT = 1.0
DAMPING = 0.6
DIAGONAL = SHIFT - 1.5 * CENTER_TAP
CELLS = 384 * 64 * 256
NORB = 4
NTYPES = 8

SIDE = tuple(-0.5 * w for w in SIDE_TAPS)
CENTER = -1.5 * CENTER_TAP
W = DAMPING / DIAGONAL
P1, P2, P3 = 3.0 * W, -3.0 * W * W, W * W * W

PL, RW, CO = 12, 16, 128
H = 6
GRAM = 32
FAR_FIRST = (10, 6, 2, 14, 11, 7, 3, 15, 8, 9, 4, 12, 5, 13, 1)
PAIRS = [(i, j) for i in range(NORB) for j in range(i + 1)]


def iota(shape, dim):
    return lax.broadcasted_iota(jnp.int32, shape, dim)


def taps_at(distance, centre):
    out = jnp.zeros(distance.shape, jnp.float32)
    if centre is not None:
        out = jnp.where(distance == 0, jnp.float32(centre), out)
    for n, w in enumerate(SIDE, 1):
        out = jnp.where(distance == n, jnp.float32(w), out)
    return out


def dot(a, b, ca, cb):
    return lax.dot_general(
        a, b, (((ca,), (cb,)), ((), ())), precision=HIGH, preferred_element_type=jnp.float32
    )


def pieces(a):
    high = a.astype(jnp.bfloat16)
    return high, (a - high.astype(jnp.float32)).astype(jnp.bfloat16)


def joined(a, axis):
    return jnp.concatenate(pieces(a), axis=axis)


def dot16(a, b, ca, cb):
    return lax.dot_general(a, b, (((ca,), (cb,)), ((), ())), preferred_element_type=jnp.float32)


def table(a):
    high, low = pieces(a)
    none = jnp.zeros(a.shape, jnp.bfloat16)
    return jnp.concatenate(
        [jnp.concatenate([high, high], axis=0), jnp.concatenate([low, none], axis=0)], axis=1
    )


def both(a):
    return a[:, :CO] + a[:, CO:]


def cholesky(s):
    low = {}
    inv = []
    for i in range(NORB):
        for j in range(i):
            t = s[i, j]
            for k in range(j):
                t = t - low[i, k] * low[j, k]
            low[i, j] = t * inv[j]
        t = s[i, i]
        for k in range(i):
            t = t - low[i, k] * low[i, k]
        root = jnp.sqrt(t)
        low[i, i] = root
        inv.append(1.0 / root)
    return low, inv


def kernel(
    x_hbm, type_hbm, table_hbm, step_hbm, out_ref,
    x_ref, type_ref, table_ref, step_ref, own_ref, pick_ref, spread_ref,
    xf, wf, nf, mf, vs, vf, base, vv, new, zz, zd_out, zd, zs, zr, gram, coef, ra, rb,
    in_sem, t_send, t_recv, d_send, d_recv, v_send, v_recv, h_send, h_recv, b_send, b_recv, r_send, r_recv,
):
    s = lax.axis_index("space")
    o = lax.axis_index("orb")
    h, c, q, x = o // 2, o % 2, s // 4, s % 4
    side = (c + q) % 2
    host = (x // 2 + q) % 2
    mine = c == host
    link = 2 * q + side
    has_left, has_right = link > 0, link < 31

    def device(hh, cc, qq, xx):
        return (2 * hh + cc, 4 * qq + xx)

    def along(n):
        n = n % 32
        return device(h, (n + n // 2) % 2, n // 2, x)

    left, right = along(link + 31), along(link + 1)
    up = device(h, c, q, (x + 3) % 4)
    down = device(h, c, q, (x + 1) % 4)
    across = device(1 - h, c, q, x)

    me1 = (x * 2 + h) * 2 + c
    me2 = q

    def peer1(k):
        i = (me1 + k) % 16
        return device((i // 2) % 2, i % 2, q, i // 4)

    def peer2(k):
        return device(h, c, (me2 + k) % 16, x)

    loads = [
        pltpu.make_async_copy(src, dst, in_sem.at[n])
        for n, (src, dst) in enumerate(
            ((x_hbm, x_ref), (type_hbm, type_ref), (table_hbm, table_ref), (step_hbm, step_ref))
        )
    ]
    for cp in loads:
        cp.start()

    barrier = pltpu.get_barrier_semaphore()

    for peer in (peer1, peer2):
        for k in FAR_FIRST:
            pl.semaphore_signal(barrier, inc=1, device_id=peer(k), device_id_type=MESH)

    def rows_of(xx):
        return pl.ds(pl.multiple_of(16 * xx, 16), 16)

    def cols_of(hh):
        return pl.ds(pl.multiple_of(CO * hh, CO), CO)

    def part(ref, xx, hh):
        return ref.at[:, rows_of(xx), cols_of(hh)]

    def remote(src, dst, ss, rs, dev):
        return pltpu.make_async_remote_copy(
            src_ref=src, dst_ref=dst, send_sem=ss, recv_sem=rs, device_id=dev, device_id_type=MESH
        )

    def guarded(cond, fn):
        if cond is None:
            fn()
        else:
            pl.when(cond)(fn)

    half = x % 2

    def scatter(j, k):
        hh, xx = (h + j) % 2, (x + k) % 4
        n = 4 * j + k
        return part(x_hbm, xx, hh), xf.at[o, pl.ds(H + 6 * half, 6), pl.ds(8, 16)], t_send.at[n], t_recv.at[2 * o + half], device(hh, host, q, xx)

    def edges(k):
        return zd_out.at[k], zd.at[c, half], d_send.at[k], d_recv.at[2 * c + half], device(h, host, q, (x + k) % 4)

    def potentials(k, n):
        xx = (x + k) % 4
        return part(vs, xx, h), vf.at[pl.ds(6 * half, 6)], v_send.at[n], v_recv.at[half], device(h, host, q, xx)

    def local_or_remote(a):
        @pl.when(mine)
        def _():
            pltpu.make_async_copy(a[0], a[1], a[3]).start()

        @pl.when(jnp.logical_not(mine))
        def _():
            remote(*a).start()

    pl.semaphore_wait(barrier, 30)

    for k in (2, 1, 3, 0):
        remote(*scatter(1, k)).start()
    for k in (2, 1, 3):
        remote(*scatter(0, k)).start()
    local_or_remote(scatter(0, 0))

    own_ref[...] = table(taps_at(jnp.abs(iota((CO, CO), 0) - iota((CO, CO), 1)), CENTER))
    row, col = iota((16, CO), 0), iota((16, CO), 1)
    target = jnp.where(row < H, CO - H + row, jnp.where(row < 2 * H, row - H, -1))
    pick = jnp.where(col == target, jnp.float32(1.0), jnp.float32(0.0)).astype(jnp.bfloat16)
    pick_ref[...] = jnp.concatenate([pick, pick], axis=1)
    spread_ref[...] = table(taps_at(
        jnp.where(row < H, col + H - row, jnp.where(row < 2 * H, CO + row - H - col, 0)), None
    ))
    gram[...] = jnp.zeros(gram.shape, jnp.float32)
    zr[:, :, :, 2 * H:] = jnp.zeros((4, 2, 3, 16 - 2 * H, CO), jnp.float32)
    for f in (xf, wf, nf, mf):
        @pl.when(jnp.logical_not(has_left))
        def _():
            f[:, 0:H] = jnp.zeros((NORB, H, RW + 16, CO), jnp.float32)

        @pl.when(jnp.logical_not(has_right))
        def _():
            f[:, H + PL:] = jnp.zeros((NORB, H, RW + 16, CO), jnp.float32)

    loads[0].wait()
    for k in range(4):
        edge = x_ref[:, rows_of((x + k) % 4), cols_of(1 - h)].reshape(6 * RW, CO)
        zd_out[k, :, 0:6 * RW] = dot16(pick_ref[...], joined(edge, 1), 1, 1)

    for k in (2, 1, 3):
        remote(*edges(k)).start()
    local_or_remote(edges(0))

    for cp in loads[1:]:
        cp.wait()
    kinds = type_ref[...]
    potential = jnp.zeros(kinds.shape, jnp.float32)
    for kind in range(NTYPES):
        potential = jnp.where(kinds == kind, table_ref[kind], potential)
    vs[...] = potential

    @pl.when(mine)
    def _():
        a = potentials(0, 0)
        pltpu.make_async_copy(a[0], a[1], a[3]).start()
        remote(*potentials(2, 1)).start()

    @pl.when(jnp.logical_not(mine))
    def _():
        remote(*potentials(1, 0)).start()
        remote(*potentials(3, 1)).start()

    A, B = h, 1 - h

    def halo_copies(f, r, pair):
        at = pl.ds(2 * pair, 2)
        m = 10 * r + 5 * pair
        return (
            (has_left, remote(f.at[at, H:2 * H, 8:8 + RW], f.at[at, H + PL:, 8:8 + RW], h_send.at[m], h_recv.at[m + 1], left)),
            (has_right, remote(f.at[at, PL:PL + H, 8:8 + RW], f.at[at, 0:H, 8:8 + RW], h_send.at[m + 1], h_recv.at[m], right)),
            (None, remote(f.at[at, H:H + PL, 8:14], f.at[at, H:H + PL, 24:30], h_send.at[m + 2], h_recv.at[m + 3], up)),
            (None, remote(f.at[at, H:H + PL, 18:24], f.at[at, H:H + PL, 2:8], h_send.at[m + 3], h_recv.at[m + 2], down)),
            (None, remote(zs.at[r, pair, :, 0:2 * H], zr.at[r, pair, :, 0:2 * H], h_send.at[m + 4], h_recv.at[m + 4], across)),
        )

    def share(f, pair):
        return f[pl.ds(2 * pair, 2), H:H + PL, 8:8 + RW].reshape(2 * PL * RW, CO)

    def halo_start(f, r, pair, with_z=True):
        copies = halo_copies(f, r, pair)
        flat = joined(share(f, pair), 1)
        if with_z:
            edge = dot16(pick_ref[...], flat, 1, 1)
            for b in range(3):
                zs[r, pair, b] = edge[:, CO * b:CO * b + CO]
            copies[4][1].start()
        for n in (0, 1, 2, 3):
            guarded(copies[n][0], copies[n][1].start)
        zz[r, pair] = both(dot16(flat, own_ref[...], 1, 0))

    def halo_finish(f, r, pair, with_z=True):
        copies = halo_copies(f, r, pair)
        guarded(has_left, copies[1][1].wait_recv)
        guarded(has_right, copies[0][1].wait_recv)
        copies[2][1].wait_recv()
        copies[3][1].wait_recv()
        if with_z == "late":
            def step(n, carry):
                at = pl.ds(pl.multiple_of(n * RW, RW), RW)
                zz[r, pair, at] = taps_xy(f, r, pair, n // PL, n % PL)
                return carry

            lax.fori_loop(0, 2 * PL, step, 0, unroll=4)
        if with_z:
            copies[4][1].wait_recv()
            zz[r, pair] += both(dot16(joined(jnp.concatenate([zr[r, pair, b] for b in range(3)], axis=1), 0), spread_ref[...], 0, 0))

    def halo_sent(f, r, pair, with_z=True):
        for cond, cp in halo_copies(f, r, pair)[:5 if with_z else 4]:
            guarded(cond, cp.wait_send)

    def kinetic(r, pair, i, p):
        return zz[r, pair, pl.ds(pl.multiple_of((i * PL + p) * RW, RW), RW)]

    def taps_xy(f, r, pair, i, p):
        total = zz[r, pair, pl.ds(pl.multiple_of((i * PL + p) * RW, RW), RW)]
        i = 2 * pair + i
        for n in range(1, H + 1):
            near = f[i, p + H + n, 8:8 + RW] + f[i, p + H - n, 8:8 + RW]
            near = near + f[i, p + H, 8 + n:8 + RW + n] + f[i, p + H, 8 - n:8 + RW - n]
            total = total + SIDE[n - 1] * near
        return total

    def each(fn, pair):
        def step(n, carry):
            fn(pair, n // PL, n % PL)
            return carry
        lax.fori_loop(0, 2 * PL, step, 0, unroll=4)

    def each_plane(fn, init=0):
        return lax.fori_loop(0, PL, fn, init, unroll=2)

    def reduce_start(v, buf, send, recv, me, peer):
        buf[me] = v

        for k in FAR_FIRST:
            remote(buf.at[me], buf.at[me], send, recv, peer(k)).start()

    def reduce_finish(buf, send, recv, peer):
        cp = remote(buf.at[pl.ds(0, 15)], buf.at[pl.ds(0, 15)], send, recv, peer(1))
        cp.wait_send()
        cp.wait_recv()
        return jnp.sum(buf[...], axis=0)

    def local_total():
        v = dot(jnp.ones((8, CO), jnp.float32), gram[...], 1, 1)[0:1]
        return jnp.concatenate([v, jnp.zeros((1, CO - GRAM), jnp.float32)], axis=1)

    def local_sums(rows):
        for n, v in enumerate(rows):
            gram[n:n + 1] = jnp.sum(v, axis=0, keepdims=True)
        return local_total()

    def spread_out(v, n):
        return jnp.broadcast_to(v[:, n:n + 1], (8, CO)) * (1.0 / CELLS)

    def wide(f, i, p):
        return f[i, p + H, 8:8 + RW].reshape(2, 8, CO)

    def narrow(f, i, p):
        return f[i, p].reshape(2, 8, CO)

    def first(pair, i, p):
        k = taps_xy(xf, 0, pair, i, p)
        i = 2 * pair + i
        v = xf[i, p + H, 8:8 + RW]
        wf[i, p + H, 8:8 + RW] = k + vf[p] * v
        nf[i, p + H, 8:8 + RW] = k + SHIFT * v

    def second(pair, i, p):
        k = taps_xy(wf, 1, pair, i, p)
        i = 2 * pair + i
        mf[i, p + H, 8:8 + RW] = k + SHIFT * wf[i, p + H, 8:8 + RW]

    def smooth_x(pair, i, p):
        k = taps_xy(nf, 2, pair, i, p)
        i = 2 * pair + i
        vv[i, p] = P1 * xf[i, p + H, 8:8 + RW] + (P2 + SHIFT * P3) * nf[i, p + H, 8:8 + RW] + P3 * k

    def smooth_w(pair, i, p):
        k = taps_xy(mf, 3, pair, i, p)
        i = 2 * pair + i
        t = P1 * wf[i, p + H, 8:8 + RW] + (P2 + SHIFT * P3) * mf[i, p + H, 8:8 + RW] + P3 * k
        base[i, p] = xf[i, p + H, 8:8 + RW] - step_ref[i] * t

    def arrived(pair):
        for i in range(2):
            for p in range(2):
                ref = xf.at[2 * pair + i, pl.ds(H + 6 * p, 6), pl.ds(8, 16)]
                remote(ref, ref, t_send.at[0], t_recv.at[2 * (2 * pair + i) + p], across).wait_recv()

    arrived(A)
    halo_start(xf, 0, A)
    arrived(B)
    halo_start(xf, 0, B, False)
    for i in range(2):
        for p in range(2):
            remote(zd.at[i, p], zd.at[i, p], d_send.at[0], d_recv.at[2 * i + p], across).wait_recv()
            at = pl.ds((2 * i + p) * 6 * RW, 6 * RW)
            zz[0, A, at] += both(dot16(joined(zd[i, p][:, 0:6 * RW], 0), spread_ref[...], 0, 0))
    for p in range(2):
        remote(vf.at[pl.ds(6 * p, 6)], vf.at[pl.ds(6 * p, 6)], v_send.at[0], v_recv.at[p], across).wait_recv()
    halo_finish(xf, 0, A, False)
    each(first, A)
    halo_start(wf, 1, A)
    halo_start(nf, 2, A)

    def products(pair, with_margin, p, acc):
        xs = [wide(xf, i, p) for i in range(NORB)]
        ws = [wide(wf, 2 * pair + i, p) for i in range(2)]
        terms = [xs[i] * xs[j] for i, j in PAIRS] if with_margin else []
        terms += [xs[j] * w for j in range(NORB) for w in ws]
        return tuple(a + jnp.sum(v, axis=0) for a, v in zip(acc, terms))

    zero = jnp.zeros((8, CO), jnp.float32)
    early = each_plane(functools.partial(products, A, True), (zero,) * 18)
    for n in range(10):
        gram[n:n + 1] = jnp.sum(early[n], axis=0, keepdims=True)
    sums = {}
    halo_finish(xf, 0, B)
    each(first, B)
    halo_start(wf, 1, B)
    acc = each_plane(functools.partial(products, B, False), (zero,) * 8)
    late = acc
    for j in range(NORB):
        for i in range(2):
            a, b = early[10 + 2 * j + i], late[2 * j + i]
            sums[10 + 4 * j + i] = jnp.where(h == 0, a, b)
            sums[12 + 4 * j + i] = jnp.where(h == 0, b, a)
    for n in range(10, 26):
        gram[n:n + 1] = jnp.sum(sums[n], axis=0, keepdims=True)
    reduce_start(local_total(), ra.at[0], r_send.at[0], r_recv.at[0], me1, peer1)
    halo_start(nf, 2, B)

    halo_finish(wf, 1, A)
    each(second, A)
    halo_start(mf, 3, A)
    halo_finish(wf, 1, B)
    each(second, B)
    halo_start(mf, 3, B)
    v = reduce_finish(ra.at[0], r_send.at[0], r_recv.at[0], peer1)
    reduce_start(v, rb.at[0], r_send.at[1], r_recv.at[1], me2, peer2)
    halo_finish(nf, 2, A)
    each(smooth_x, A)
    halo_finish(nf, 2, B)
    each(smooth_x, B)
    halo_finish(mf, 3, A)
    each(smooth_w, A)
    halo_finish(mf, 3, B)
    each(smooth_w, B)

    v = reduce_finish(rb.at[0], r_send.at[1], r_recv.at[1], peer2)
    margin = {(i, j): spread_out(v, n) for n, (i, j) in enumerate(PAIRS)}
    low, inv = cholesky(margin)
    for i in range(NORB):
        y = []
        for j in range(NORB):
            t = spread_out(v, 10 + 4 * j + i)
            for k in range(j):
                t = t - low[j, k] * y[k]
            y.append(t * inv[j])
        for j in reversed(range(NORB)):
            t = y[j]
            for k in range(j + 1, NORB):
                t = t - low[k, j] * y[k]
            y[j] = t * inv[j]
            coef[4 * i + j] = step_ref[i] * y[j]

    def move(p, acc):
        vs4 = [narrow(vv, j, p) for j in range(NORB)]
        ms = []
        for i in range(NORB):
            t = narrow(base, i, p)
            for j in range(NORB):
                t = t + coef[4 * i + j] * vs4[j]
            base[i, p] = t.reshape(RW, CO)
            ms.append(t)
        return tuple(a + jnp.sum(ms[i] * ms[j], axis=0) for a, (i, j) in zip(acc, PAIRS))

    acc = each_plane(move, (zero,) * 10)
    reduce_start(local_sums(acc), ra.at[1], r_send.at[2], r_recv.at[2], me1, peer1)
    v = reduce_finish(ra.at[1], r_send.at[2], r_recv.at[2], peer1)
    reduce_start(v, rb.at[1], r_send.at[3], r_recv.at[3], me2, peer2)
    v = reduce_finish(rb.at[1], r_send.at[3], r_recv.at[3], peer2)
    low, inv = cholesky({(i, j): spread_out(v, n) for n, (i, j) in enumerate(PAIRS)})
    lowinv = {}
    for j in range(NORB):
        lowinv[j, j] = inv[j]
        for i in range(j + 1, NORB):
            t = low[i, j] * lowinv[j, j]
            for k in range(j + 1, i):
                t = t + low[i, k] * lowinv[k, j]
            lowinv[i, j] = -t * inv[i]
    for n, ij in enumerate(PAIRS):
        coef[n] = lowinv[ij]

    def rotate(p):
        ms = [narrow(base, j, p) for j in range(NORB)]
        for i in range(NORB):
            t = None
            for n, (a, j) in enumerate(PAIRS):
                if a == i:
                    term = coef[n] * ms[j]
                    t = term if t is None else t + term
            new[i, p] = t.reshape(RW, CO)

    def back(j, i, m):
        hh, cc, pp = (h + j) % 2, (c + i) % 2, (x + m) % 2
        return new.at[2 * hh + cc, pl.ds(6 * pp, 6)], part(out_ref, x, h), b_send.at[4 * j + 2 * i + m], b_recv.at[2 * x + h], device(hh, cc, q, 2 * side + pp)

    order = [(j, i, m) for j in (1, 0) for i in (1, 0) for m in (1, 0)]
    for m in (1, 0):
        for p in range(6):
            rotate(6 * ((x + m) % 2) + p)
        for i in (1, 0):
            remote(*back(1, i, m)).start()
    for jim in order[4:]:
        if jim == (0, 0, 0):
            local_or_remote(back(*jim))
        else:
            remote(*back(*jim)).start()

    unless_mine = jnp.logical_not(mine)
    for k in range(4):
        remote(*scatter(1, k)).wait_send()
        guarded(unless_mine if k == 0 else None, remote(*scatter(0, k)).wait_send)
        guarded(unless_mine if k == 0 else None, remote(*edges(k)).wait_send)

    @pl.when(mine)
    def _():
        remote(*potentials(2, 1)).wait_send()

    @pl.when(unless_mine)
    def _():
        remote(*potentials(1, 0)).wait_send()
        remote(*potentials(3, 1)).wait_send()

    for r, f in enumerate((xf, wf, nf, mf)):
        halo_sent(f, r, A)
        halo_sent(f, r, B, r > 0)
    for jim in order:
        guarded(unless_mine if jim == (0, 0, 0) else None, remote(*back(*jim)).wait_send)
    for xx in range(4):
        for hh in range(2):
            dst = out_ref.at[:, pl.ds(16 * xx, 16), pl.ds(CO * hh, CO)]
            remote(dst, dst, b_send.at[0], b_recv.at[2 * xx + hh], across).wait_recv()


def body(orbitals, atom_type, type_table, step_length):
    shape = orbitals.shape
    slab = shape[1:]
    anywhere = pl.BlockSpec(memory_space=pl.ANY)
    f32 = jnp.float32
    share = (NORB, PL, RW, CO)
    wide = (NORB, PL + 2 * H, RW + 16, CO)
    rows = 2 * PL * RW
    dma = pltpu.SemaphoreType.DMA

    def vmem(*shape):
        return pltpu.VMEM(shape, f32)

    out = pl.pallas_call(
        kernel,
        out_shape=jax.ShapeDtypeStruct(slab, f32),
        in_specs=[anywhere] * 4,
        out_specs=pl.BlockSpec(memory_space=pltpu.VMEM),
        scratch_shapes=[
            vmem(*slab), pltpu.VMEM(slab, jnp.int32), pltpu.SMEM((NTYPES,), f32), pltpu.SMEM((NORB,), f32),
            pltpu.VMEM((2 * CO, 2 * CO), jnp.bfloat16), pltpu.VMEM((16, 2 * CO), jnp.bfloat16), pltpu.VMEM((32, 2 * CO), jnp.bfloat16),
            vmem(*wide), vmem(*wide), vmem(*wide), vmem(*wide),
            vmem(*slab), vmem(PL, RW, CO), vmem(*share), vmem(*share), vmem(*share),
            vmem(4, 2, rows, CO), vmem(4, 16, CO), vmem(2, 2, 16, CO),
            vmem(4, 2, 3, 16, CO), vmem(4, 2, 3, 16, CO),
            vmem(GRAM, CO), vmem(16, 8, CO), vmem(2, 16, 1, CO), vmem(2, 16, 1, CO),
            dma((4,)), dma((8,)), dma((8,)), dma((4,)), dma((4,)), dma((2,)), dma((2,)),
            dma((40,)), dma((40,)), dma((8,)), dma((8,)), dma((4,)), dma((4,)),
        ],
        compiler_params=pltpu.CompilerParams(
            collective_id=0, has_side_effects=True, vmem_limit_bytes=55993958
        ),
        name="step",
    )(orbitals.reshape(slab), atom_type, type_table, step_length)
    return out.reshape(shape)


def solution(mesh):
    in_specs = (P("orb", "space", None, None), P("space", None, None), P(), P())
    out_specs = P("orb", "space", None, None)
    return jax.shard_map(body, mesh=mesh, in_specs=in_specs, out_specs=out_specs, check_vma=False)
```

```python
import functools

import jax
import jax.numpy as jnp
from jax import lax
from jax.experimental import pallas as pl
from jax.experimental.pallas import tpu as pltpu
from jax.sharding import PartitionSpec as P

MESH = pl.DeviceIdType.MESH
HIGH = lax.Precision.HIGHEST
CENTER_TAP = -5369.0 / 1800.0
SIDE_TAPS = (12.0 / 7.0, -15.0 / 56.0, 10.0 / 189.0, -1.0 / 112.0, 2.0 / 1925.0, -1.0 / 16632.0)
SHIFT = 1.0
DAMPING = 0.6
DIAGONAL = SHIFT - 1.5 * CENTER_TAP
CELLS = 384 * 64 * 256
NORB = 4
NTYPES = 8

SIDE = tuple(-0.5 * w for w in SIDE_TAPS)
CENTER = -1.5 * CENTER_TAP
W = DAMPING / DIAGONAL
P1, P2, P3 = 3.0 * W, -3.0 * W * W, W * W * W

PL, RW, CO = 12, 16, 128
H = 6
GRAM = 32
AHEAD = 3
FAR_FIRST = (10, 6, 2, 14, 11, 7, 3, 15, 8, 9, 4, 12, 5, 13, 1)
PAIRS = [(i, j) for i in range(NORB) for j in range(i + 1)]


def iota(shape, dim):
    return lax.broadcasted_iota(jnp.int32, shape, dim)


def taps_at(distance, centre):
    out = jnp.zeros(distance.shape, jnp.float32)
    if centre is not None:
        out = jnp.where(distance == 0, jnp.float32(centre), out)
    for n, w in enumerate(SIDE, 1):
        out = jnp.where(distance == n, jnp.float32(w), out)
    return out


def dot(a, b, ca, cb):
    return lax.dot_general(
        a, b, (((ca,), (cb,)), ((), ())), precision=HIGH, preferred_element_type=jnp.float32
    )


def pieces(a):
    high = a.astype(jnp.bfloat16)
    return high, (a - high.astype(jnp.float32)).astype(jnp.bfloat16)


def joined(a, axis):
    return jnp.concatenate(pieces(a), axis=axis)


def dot16(a, b, ca, cb):
    return lax.dot_general(a, b, (((ca,), (cb,)), ((), ())), preferred_element_type=jnp.float32)


def table(a):
    high, low = pieces(a)
    none = jnp.zeros(a.shape, jnp.bfloat16)
    return jnp.concatenate(
        [jnp.concatenate([high, high], axis=0), jnp.concatenate([low, none], axis=0)], axis=1
    )


def both(a):
    return a[:, :CO] + a[:, CO:]


def cholesky(s):
    low = {}
    inv = []
    for i in range(NORB):
        for j in range(i):
            t = s[i, j]
            for k in range(j):
                t = t - low[i, k] * low[j, k]
            low[i, j] = t * inv[j]
        t = s[i, i]
        for k in range(i):
            t = t - low[i, k] * low[i, k]
        root = jnp.sqrt(t)
        low[i, i] = root
        inv.append(1.0 / root)
    return low, inv


def kernel(
    x_hbm, type_hbm, table_hbm, step_hbm, out_ref,
    x_ref, type_ref, table_ref, step_ref, own_ref, pick_ref, spread_ref,
    xf, wf, nf, mf, vs, vf, base, vv, new, zz, zd_out, zd, zs, zr, gram, coef, ra, rb,
    in_sem, t_send, t_recv, d_send, d_recv, v_send, v_recv, h_send, h_recv, b_send, b_recv, r_send, r_recv,
    e_send, e_recv, f_send, f_recv, eb,
):
    s = lax.axis_index("space")
    o = lax.axis_index("orb")
    h, c, q, x = o // 2, o % 2, s // 4, s % 4
    side = (c + q) % 2
    host = (x // 2 + q) % 2
    mine = c == host
    link = 2 * q + side
    has_left, has_right = link > 0, link < 31

    def device(hh, cc, qq, xx):
        return (2 * hh + cc, 4 * qq + xx)

    def along(n):
        n = n % 32
        return device(h, (n + n // 2) % 2, n // 2, x)

    left, right = along(link + 31), along(link + 1)
    up = device(h, c, q, (x + 3) % 4)
    down = device(h, c, q, (x + 1) % 4)
    across = device(1 - h, c, q, x)

    me1 = (x * 2 + h) * 2 + c
    me2 = q

    def peer1(k):
        i = (me1 + k) % 16
        return device((i // 2) % 2, i % 2, q, i // 4)

    def peer2(k):
        return device(h, c, (me2 + k) % 16, x)

    loads = [
        pltpu.make_async_copy(src, dst, in_sem.at[n])
        for n, (src, dst) in enumerate(
            ((x_hbm, x_ref), (type_hbm, type_ref), (table_hbm, table_ref), (step_hbm, step_ref))
        )
    ]
    for cp in loads:
        cp.start()

    barrier = pltpu.get_barrier_semaphore()

    for peer in (peer1, peer2):
        for k in FAR_FIRST:
            pl.semaphore_signal(barrier, inc=1, device_id=peer(k), device_id_type=MESH)

    def rows_of(xx):
        return pl.ds(pl.multiple_of(16 * xx, 16), 16)

    def cols_of(hh):
        return pl.ds(pl.multiple_of(CO * hh, CO), CO)

    def part(ref, xx, hh):
        return ref.at[:, rows_of(xx), cols_of(hh)]

    def remote(src, dst, ss, rs, dev):
        return pltpu.make_async_remote_copy(
            src_ref=src, dst_ref=dst, send_sem=ss, recv_sem=rs, device_id=dev, device_id_type=MESH
        )

    def guarded(cond, fn):
        if cond is None:
            fn()
        else:
            pl.when(cond)(fn)

    half = x % 2

    def scatter(j, k):
        hh, xx = (h + j) % 2, (x + k) % 4
        n = 4 * j + k
        return part(x_hbm, xx, hh), xf.at[o, pl.ds(H + 6 * half, 6), pl.ds(8, 16)], t_send.at[n], t_recv.at[2 * o + half], device(hh, host, q, xx)

    def edges(k):
        return zd_out.at[k], zd.at[c, half], d_send.at[k], d_recv.at[2 * c + half], device(h, host, q, (x + k) % 4)

    def potentials(k, n):
        xx = (x + k) % 4
        return part(vs, xx, h), vf.at[pl.ds(6 * half, 6)], v_send.at[n], v_recv.at[half], device(h, host, q, xx)

    def local_or_remote(a):
        @pl.when(mine)
        def _():
            pltpu.make_async_copy(a[0], a[1], a[3]).start()

        @pl.when(jnp.logical_not(mine))
        def _():
            remote(*a).start()

    pl.semaphore_wait(barrier, 30)

    for k in (2, 1, 3, 0):
        remote(*scatter(1, k)).start()
    for k in (2, 1, 3):
        remote(*scatter(0, k)).start()
    local_or_remote(scatter(0, 0))

    own_ref[...] = table(taps_at(jnp.abs(iota((CO, CO), 0) - iota((CO, CO), 1)), CENTER))
    row, col = iota((16, CO), 0), iota((16, CO), 1)
    target = jnp.where(row < H, CO - H + row, jnp.where(row < 2 * H, row - H, -1))
    pick = jnp.where(col == target, jnp.float32(1.0), jnp.float32(0.0)).astype(jnp.bfloat16)
    pick_ref[...] = jnp.concatenate([pick, pick], axis=1)
    spread_ref[...] = table(taps_at(
        jnp.where(row < H, col + H - row, jnp.where(row < 2 * H, CO + row - H - col, 0)), None
    ))
    gram[...] = jnp.zeros(gram.shape, jnp.float32)
    zr[:, :, :, 2 * H:] = jnp.zeros((4, 2, 3, 16 - 2 * H, CO), jnp.float32)
    for f in (xf, wf, nf, mf):
        @pl.when(jnp.logical_not(has_left))
        def _():
            f[:, 0:H] = jnp.zeros((NORB, H, RW + 16, CO), jnp.float32)

        @pl.when(jnp.logical_not(has_right))
        def _():
            f[:, H + PL:] = jnp.zeros((NORB, H, RW + 16, CO), jnp.float32)

    loads[0].wait()
    for k in range(4):
        edge = x_ref[:, rows_of((x + k) % 4), cols_of(1 - h)].reshape(6 * RW, CO)
        zd_out[k, :, 0:6 * RW] = dot16(pick_ref[...], joined(edge, 1), 1, 1)

    for k in (2, 1, 3):
        remote(*edges(k)).start()
    local_or_remote(edges(0))

    for cp in loads[1:]:
        cp.wait()
    kinds = type_ref[...]
    potential = jnp.zeros(kinds.shape, jnp.float32)
    for kind in range(NTYPES):
        potential = jnp.where(kinds == kind, table_ref[kind], potential)
    vs[...] = potential

    @pl.when(mine)
    def _():
        a = potentials(0, 0)
        pltpu.make_async_copy(a[0], a[1], a[3]).start()
        remote(*potentials(2, 1)).start()

    @pl.when(jnp.logical_not(mine))
    def _():
        remote(*potentials(1, 0)).start()
        remote(*potentials(3, 1)).start()

    A, B = h, 1 - h

    def halo_copies(f, r, pair):
        at = pl.ds(2 * pair, 2)
        m = 10 * r + 5 * pair
        return (
            (has_left, remote(f.at[at, H:2 * H, 8:8 + RW], f.at[at, H + PL:, 8:8 + RW], h_send.at[m], h_recv.at[m + 1], left)),
            (has_right, remote(f.at[at, PL:PL + H, 8:8 + RW], f.at[at, 0:H, 8:8 + RW], h_send.at[m + 1], h_recv.at[m], right)),
            (None, remote(f.at[at, H:H + PL, 8:14], f.at[at, H:H + PL, 24:30], h_send.at[m + 2], h_recv.at[m + 3], up)),
            (None, remote(f.at[at, H:H + PL, 18:24], f.at[at, H:H + PL, 2:8], h_send.at[m + 3], h_recv.at[m + 2], down)),
            (None, remote(zs.at[r, pair, :, 0:2 * H], zr.at[r, pair, :, 0:2 * H], h_send.at[m + 4], h_recv.at[m + 4], across)),
        )

    def share(f, pair):
        return f[pl.ds(2 * pair, 2), H:H + PL, 8:8 + RW].reshape(2 * PL * RW, CO)

    def halo_start(f, r, pair, with_z=True):
        copies = halo_copies(f, r, pair)
        flat = joined(share(f, pair), 1)
        if with_z:
            edge = dot16(pick_ref[...], flat, 1, 1)
            for b in range(3):
                zs[r, pair, b] = edge[:, CO * b:CO * b + CO]
            copies[4][1].start()
        for n in (0, 1, 2, 3):
            guarded(copies[n][0], copies[n][1].start)
        zz[r, pair] = both(dot16(flat, own_ref[...], 1, 0))

    def halo_finish(f, r, pair, with_z=True):
        copies = halo_copies(f, r, pair)
        guarded(has_left, copies[1][1].wait_recv)
        guarded(has_right, copies[0][1].wait_recv)
        copies[2][1].wait_recv()
        copies[3][1].wait_recv()
        if with_z == "late":
            def step(n, carry):
                at = pl.ds(pl.multiple_of(n * RW, RW), RW)
                zz[r, pair, at] = taps_xy(f, r, pair, n // PL, n % PL)
                return carry

            lax.fori_loop(0, 2 * PL, step, 0, unroll=4)
        if with_z:
            copies[4][1].wait_recv()
            zz[r, pair] += both(dot16(joined(jnp.concatenate([zr[r, pair, b] for b in range(3)], axis=1), 0), spread_ref[...], 0, 0))

    def halo_sent(f, r, pair, with_z=True):
        for cond, cp in halo_copies(f, r, pair)[:5 if with_z else 4]:
            guarded(cond, cp.wait_send)

    def kinetic(r, pair, i, p):
        return zz[r, pair, pl.ds(pl.multiple_of((i * PL + p) * RW, RW), RW)]

    def taps_xy(f, r, pair, i, p):
        total = zz[r, pair, pl.ds(pl.multiple_of((i * PL + p) * RW, RW), RW)]
        i = 2 * pair + i
        for n in range(1, H + 1):
            near = f[i, p + H + n, 8:8 + RW] + f[i, p + H - n, 8:8 + RW]
            near = near + f[i, p + H, 8 + n:8 + RW + n] + f[i, p + H, 8 - n:8 + RW - n]
            total = total + SIDE[n - 1] * near
        return total

    def each(fn, pair):
        def step(n, carry):
            fn(pair, n // PL, n % PL)
            return carry
        lax.fori_loop(0, 2 * PL, step, 0, unroll=4)

    def each_plane(fn, init=0):
        return lax.fori_loop(0, PL, fn, init, unroll=2)

    def reduce_start(v, buf, send, recv, me, peer):
        buf[me] = v

        for k in FAR_FIRST:
            remote(buf.at[me], buf.at[me], send, recv, peer(k)).start()

    def reduce_finish(buf, send, recv, peer):
        cp = remote(buf.at[pl.ds(0, 15)], buf.at[pl.ds(0, 15)], send, recv, peer(1))
        cp.wait_send()
        cp.wait_recv()
        return jnp.sum(buf[...], axis=0)

    def local_total():
        v = dot(jnp.ones((8, CO), jnp.float32), gram[...], 1, 1)[0:1]
        return jnp.concatenate([v, jnp.zeros((1, CO - GRAM), jnp.float32)], axis=1)

    def local_sums(rows):
        for n, v in enumerate(rows):
            gram[n:n + 1] = jnp.sum(v, axis=0, keepdims=True)
        return local_total()

    def spread_out(v, n):
        return jnp.broadcast_to(v[:, n:n + 1], (8, CO)) * (1.0 / CELLS)

    def wide(f, i, p):
        return f[i, p + H, 8:8 + RW].reshape(2, 8, CO)

    def narrow(f, i, p):
        return f[i, p].reshape(2, 8, CO)

    def first(pair, i, p):
        k = taps_xy(xf, 0, pair, i, p)
        i = 2 * pair + i
        v = xf[i, p + H, 8:8 + RW]
        wf[i, p + H, 8:8 + RW] = k + vf[p] * v
        nf[i, p + H, 8:8 + RW] = k + SHIFT * v

    def second(pair, i, p):
        k = taps_xy(wf, 1, pair, i, p)
        i = 2 * pair + i
        mf[i, p + H, 8:8 + RW] = k + SHIFT * wf[i, p + H, 8:8 + RW]

    def smooth_x(pair, i, p):
        k = taps_xy(nf, 2, pair, i, p)
        i = 2 * pair + i
        vv[i, p] = P1 * xf[i, p + H, 8:8 + RW] + (P2 + SHIFT * P3) * nf[i, p + H, 8:8 + RW] + P3 * k

    def smooth_w(pair, i, p):
        k = taps_xy(mf, 3, pair, i, p)
        i = 2 * pair + i
        t = P1 * wf[i, p + H, 8:8 + RW] + (P2 + SHIFT * P3) * mf[i, p + H, 8:8 + RW] + P3 * k
        base[i, p] = xf[i, p + H, 8:8 + RW] - step_ref[i] * t

    def arrived(pair):
        for i in range(2):
            for p in range(2):
                ref = xf.at[2 * pair + i, pl.ds(H + 6 * p, 6), pl.ds(8, 16)]
                remote(ref, ref, t_send.at[0], t_recv.at[2 * (2 * pair + i) + p], across).wait_recv()

    arrived(A)
    halo_start(xf, 0, A)
    arrived(B)
    halo_start(xf, 0, B, False)
    for i in range(2):
        for p in range(2):
            remote(zd.at[i, p], zd.at[i, p], d_send.at[0], d_recv.at[2 * i + p], across).wait_recv()
            at = pl.ds((2 * i + p) * 6 * RW, 6 * RW)
            zz[0, A, at] += both(dot16(joined(zd[i, p][:, 0:6 * RW], 0), spread_ref[...], 0, 0))
    for p in range(2):
        remote(vf.at[pl.ds(6 * p, 6)], vf.at[pl.ds(6 * p, 6)], v_send.at[0], v_recv.at[p], across).wait_recv()
    halo_finish(xf, 0, A, False)
    each(first, A)
    halo_start(wf, 1, A)
    halo_start(nf, 2, A)

    def products(pair, with_margin, p, acc):
        xs = [wide(xf, i, p) for i in range(NORB)]
        ws = [wide(wf, 2 * pair + i, p) for i in range(2)]
        terms = [xs[i] * xs[j] for i, j in PAIRS] if with_margin else []
        terms += [xs[j] * w for j in range(NORB) for w in ws]
        return tuple(a + jnp.sum(v, axis=0) for a, v in zip(acc, terms))

    zero = jnp.zeros((8, CO), jnp.float32)
    early = each_plane(functools.partial(products, A, True), (zero,) * 18)
    for n in range(10):
        gram[n:n + 1] = jnp.sum(early[n], axis=0, keepdims=True)
    sums = {}
    halo_finish(xf, 0, B)
    each(first, B)
    halo_start(wf, 1, B)
    acc = each_plane(functools.partial(products, B, False), (zero,) * 8)
    late = acc
    for j in range(NORB):
        for i in range(2):
            a, b = early[10 + 2 * j + i], late[2 * j + i]
            sums[10 + 4 * j + i] = jnp.where(h == 0, a, b)
            sums[12 + 4 * j + i] = jnp.where(h == 0, b, a)
    for n in range(10, 26):
        gram[n:n + 1] = jnp.sum(sums[n], axis=0, keepdims=True)
    reduce_start(local_total(), ra.at[0], r_send.at[0], r_recv.at[0], me1, peer1)
    halo_start(nf, 2, B)

    halo_finish(wf, 1, A)
    each(second, A)
    halo_start(mf, 3, A)
    halo_finish(wf, 1, B)
    each(second, B)
    halo_start(mf, 3, B)
    v = reduce_finish(ra.at[0], r_send.at[0], r_recv.at[0], peer1)
    reduce_start(v, rb.at[0], r_send.at[1], r_recv.at[1], me2, peer2)
    halo_finish(nf, 2, A)
    each(smooth_x, A)
    halo_finish(nf, 2, B)
    each(smooth_x, B)
    halo_finish(mf, 3, A)
    each(smooth_w, A)
    halo_finish(mf, 3, B)
    each(smooth_w, B)

    v = reduce_finish(rb.at[0], r_send.at[1], r_recv.at[1], peer2)
    margin = {(i, j): spread_out(v, n) for n, (i, j) in enumerate(PAIRS)}
    low, inv = cholesky(margin)
    for i in range(NORB):
        y = []
        for j in range(NORB):
            t = spread_out(v, 10 + 4 * j + i)
            for k in range(j):
                t = t - low[j, k] * y[k]
            y.append(t * inv[j])
        for j in reversed(range(NORB)):
            t = y[j]
            for k in range(j + 1, NORB):
                t = t - low[k, j] * y[k]
            y[j] = t * inv[j]
            coef[4 * i + j] = step_ref[i] * y[j]

    def move(p, acc):
        vs4 = [narrow(vv, j, p) for j in range(NORB)]
        ms = []
        for i in range(NORB):
            t = narrow(base, i, p)
            for j in range(NORB):
                t = t + coef[4 * i + j] * vs4[j]
            base[i, p] = t.reshape(RW, CO)
            ms.append(t)
        return tuple(a + jnp.sum(ms[i] * ms[j], axis=0) for a, (i, j) in zip(acc, PAIRS))

    acc = each_plane(move, (zero,) * 10)
    reduce_start(local_sums(acc), ra.at[1], r_send.at[2], r_recv.at[2], me2, peer2)

    high = h == 1

    def ahead(f, m):
        pp = (x + m) % 2
        return base.at[f, pl.ds(6 * pp, AHEAD)], eb.at[f, :, rows_of(x)], e_send.at[2 * f + m], e_recv.at[4 * f + x], device(1 - h, f % 2, q, 2 * side + pp)

    for f in range(NORB):
        for m in (1, 0):
            guarded(None if f < 2 else jnp.logical_not(high), remote(*ahead(f, m)).start)
    v = reduce_finish(ra.at[1], r_send.at[2], r_recv.at[2], peer2)
    reduce_start(v, rb.at[1], r_send.at[3], r_recv.at[3], me1, peer1)
    v = reduce_finish(rb.at[1], r_send.at[3], r_recv.at[3], peer1)
    low, inv = cholesky({(i, j): spread_out(v, n) for n, (i, j) in enumerate(PAIRS)})
    lowinv = {}
    for j in range(NORB):
        lowinv[j, j] = inv[j]
        for i in range(j + 1, NORB):
            t = low[i, j] * lowinv[j, j]
            for k in range(j + 1, i):
                t = t + low[i, k] * lowinv[k, j]
            lowinv[i, j] = -t * inv[i]
    for n, ij in enumerate(PAIRS):
        coef[n] = lowinv[ij]

    def rotate(p):
        ms = [narrow(base, j, p) for j in range(NORB)]
        for i in range(NORB):
            t = None
            for n, (a, j) in enumerate(PAIRS):
                if a == i:
                    term = coef[n] * ms[j]
                    t = term if t is None else t + term
            new[i, p] = t.reshape(RW, CO)

    def back(j, i, m):
        hh, cc, pp = (h + j) % 2, (c + i) % 2, (x + m) % 2
        n = 4 * j + 2 * i + m
        src, dst = new.at[2 * hh + cc, pl.ds(6 * pp + AHEAD * j, 6 - AHEAD * j)], part(out_ref, x, h).at[pl.ds(AHEAD * j, 6 - AHEAD * j)]
        return src, dst, b_send.at[n], b_recv.at[2 * x + h], device(hh, cc, q, 2 * side + pp)

    order = [(j, i, m) for j in (1, 0) for i in (1, 0) for m in (1, 0)]
    for m in (1, 0):
        for p in range(AHEAD, 6):
            rotate(6 * ((x + m) % 2) + p)
        for i in (1, 0):
            remote(*back(1, i, m)).start()
    for p in range(AHEAD):
        rotate(p)
        rotate(6 + p)
    for jim in order[4:]:
        if jim == (0, 0, 0):
            local_or_remote(back(*jim))
        else:
            remote(*back(*jim)).start()

    def came(f):
        for xx in range(4):
            ref = eb.at[f, :, pl.ds(16 * xx, 16)]
            remote(ref, ref, e_send.at[0], e_recv.at[4 * f + xx], across).wait_recv()

    def pass_on(f):
        return remote(eb.at[f], eb.at[f], f_send.at[f], f_recv.at[f], device(h, 1 - c, q, x))

    gives = {0: c == 0, 1: jnp.logical_and(c == 1, high), 2: jnp.logical_and(c == 0, high)}
    takes = {0: c == 1, 1: jnp.logical_and(c == 0, high), 2: jnp.logical_and(c == 1, high)}
    for f in range(NORB):
        @pl.when(jnp.logical_and(c == f % 2, high) if f > 1 else c == f % 2)
        def _():
            came(f)

        if f < 3:
            guarded(gives[f], pass_on(f).start)
    for f in range(3):
        guarded(takes[f], pass_on(f).wait_recv)
    for i in range(NORB):
        @pl.when(o == i)
        def _():
            t = None
            for n, (a, j) in enumerate(PAIRS):
                if a == i:
                    term = coef[n] * eb[j].reshape(8 * AHEAD, 8, CO)
                    t = term if t is None else t + term
            out_ref[0:AHEAD, :, cols_of(1 - h)] = t.reshape(AHEAD, 64, CO)

    unless_mine = jnp.logical_not(mine)
    for k in range(4):
        remote(*scatter(1, k)).wait_send()
        guarded(unless_mine if k == 0 else None, remote(*scatter(0, k)).wait_send)
        guarded(unless_mine if k == 0 else None, remote(*edges(k)).wait_send)

    @pl.when(mine)
    def _():
        remote(*potentials(2, 1)).wait_send()

    @pl.when(unless_mine)
    def _():
        remote(*potentials(1, 0)).wait_send()
        remote(*potentials(3, 1)).wait_send()

    for r, f in enumerate((xf, wf, nf, mf)):
        halo_sent(f, r, A)
        halo_sent(f, r, B, r > 0)
    for jim in order:
        guarded(unless_mine if jim == (0, 0, 0) else None, remote(*back(*jim)).wait_send)
    for f in range(NORB):
        for m in (1, 0):
            guarded(None if f < 2 else jnp.logical_not(high), remote(*ahead(f, m)).wait_send)
    for f in range(3):
        guarded(gives[f], pass_on(f).wait_send)
    for xx in range(4):
        dst = part(out_ref, xx, h)
        remote(dst, dst, b_send.at[0], b_recv.at[2 * xx + h], across).wait_recv()
        dst = part(out_ref, xx, 1 - h).at[pl.ds(AHEAD, 6 - AHEAD)]
        remote(dst, dst, b_send.at[0], b_recv.at[2 * xx + 1 - h], across).wait_recv()


def body(orbitals, atom_type, type_table, step_length):
    shape = orbitals.shape
    slab = shape[1:]
    anywhere = pl.BlockSpec(memory_space=pl.ANY)
    f32 = jnp.float32
    share = (NORB, PL, RW, CO)
    wide = (NORB, PL + 2 * H, RW + 16, CO)
    rows = 2 * PL * RW
    dma = pltpu.SemaphoreType.DMA

    def vmem(*shape):
        return pltpu.VMEM(shape, f32)

    out = pl.pallas_call(
        kernel,
        out_shape=jax.ShapeDtypeStruct(slab, f32),
        in_specs=[anywhere] * 4,
        out_specs=pl.BlockSpec(memory_space=pltpu.VMEM),
        scratch_shapes=[
            vmem(*slab), pltpu.VMEM(slab, jnp.int32), pltpu.SMEM((NTYPES,), f32), pltpu.SMEM((NORB,), f32),
            pltpu.VMEM((2 * CO, 2 * CO), jnp.bfloat16), pltpu.VMEM((16, 2 * CO), jnp.bfloat16), pltpu.VMEM((32, 2 * CO), jnp.bfloat16),
            vmem(*wide), vmem(*wide), vmem(*wide), vmem(*wide),
            vmem(*slab), vmem(PL, RW, CO), vmem(*share), vmem(*share), vmem(*share),
            vmem(4, 2, rows, CO), vmem(4, 16, CO), vmem(2, 2, 16, CO),
            vmem(4, 2, 3, 16, CO), vmem(4, 2, 3, 16, CO),
            vmem(GRAM, CO), vmem(16, 8, CO), vmem(2, 16, 1, CO), vmem(2, 16, 1, CO),
            dma((4,)), dma((8,)), dma((8,)), dma((4,)), dma((4,)), dma((2,)), dma((2,)),
            dma((40,)), dma((40,)), dma((8,)), dma((8,)), dma((4,)), dma((4,)),
            dma((8,)), dma((16,)), dma((3,)), dma((3,)), vmem(NORB, AHEAD, 64, CO),
        ],
        compiler_params=pltpu.CompilerParams(
            collective_id=0, has_side_effects=True, vmem_limit_bytes=55993958
        ),
        name="step",
    )(orbitals.reshape(slab), atom_type, type_table, step_length)
    return out.reshape(shape)


def solution(mesh):
    in_specs = (P("orb", "space", None, None), P("space", None, None), P(), P())
    out_specs = P("orb", "space", None, None)
    return jax.shard_map(body, mesh=mesh, in_specs=in_specs, out_specs=out_specs, check_vma=False)
```

```python
import functools

import jax
import jax.numpy as jnp
from jax import lax
from jax.experimental import pallas as pl
from jax.experimental.pallas import tpu as pltpu
from jax.sharding import PartitionSpec as P

MESH = pl.DeviceIdType.MESH
HIGH = lax.Precision.HIGHEST
CENTER_TAP = -5369.0 / 1800.0
SIDE_TAPS = (12.0 / 7.0, -15.0 / 56.0, 10.0 / 189.0, -1.0 / 112.0, 2.0 / 1925.0, -1.0 / 16632.0)
SHIFT = 1.0
DAMPING = 0.6
DIAGONAL = SHIFT - 1.5 * CENTER_TAP
CELLS = 384 * 64 * 256
NORB = 4
NTYPES = 8

SIDE = tuple(-0.5 * w for w in SIDE_TAPS)
CENTER = -1.5 * CENTER_TAP
W = DAMPING / DIAGONAL
P1, P2, P3 = 3.0 * W, -3.0 * W * W, W * W * W

PL, RW, CO = 12, 16, 128
H = 6
GRAM = 32
AHEAD = 3
FAR_FIRST = (10, 6, 2, 14, 11, 7, 3, 15, 8, 9, 4, 12, 5, 13, 1)
PAIRS = [(i, j) for i in range(NORB) for j in range(i + 1)]


def iota(shape, dim):
    return lax.broadcasted_iota(jnp.int32, shape, dim)


def taps_at(distance, centre):
    out = jnp.zeros(distance.shape, jnp.float32)
    if centre is not None:
        out = jnp.where(distance == 0, jnp.float32(centre), out)
    for n, w in enumerate(SIDE, 1):
        out = jnp.where(distance == n, jnp.float32(w), out)
    return out


def dot(a, b, ca, cb):
    return lax.dot_general(
        a, b, (((ca,), (cb,)), ((), ())), precision=HIGH, preferred_element_type=jnp.float32
    )


def pieces(a):
    high = a.astype(jnp.bfloat16)
    return high, (a - high.astype(jnp.float32)).astype(jnp.bfloat16)


def joined(a, axis):
    return jnp.concatenate(pieces(a), axis=axis)


def dot16(a, b, ca, cb):
    return lax.dot_general(a, b, (((ca,), (cb,)), ((), ())), preferred_element_type=jnp.float32)


def table(a):
    high, low = pieces(a)
    none = jnp.zeros(a.shape, jnp.bfloat16)
    return jnp.concatenate(
        [jnp.concatenate([high, high], axis=0), jnp.concatenate([low, none], axis=0)], axis=1
    )


def both(a):
    return a[:, :CO] + a[:, CO:]


def cholesky(s):
    low = {}
    inv = []
    for i in range(NORB):
        for j in range(i):
            t = s[i, j]
            for k in range(j):
                t = t - low[i, k] * low[j, k]
            low[i, j] = t * inv[j]
        t = s[i, i]
        for k in range(i):
            t = t - low[i, k] * low[i, k]
        root = jnp.sqrt(t)
        low[i, i] = root
        inv.append(1.0 / root)
    return low, inv


def kernel(
    x_hbm, type_hbm, table_hbm, step_hbm, out_ref,
    x_ref, type_ref, table_ref, step_ref, own_ref, pick_ref, spread_ref,
    xf, wf, nf, mf, vs, vf, base, vv, new, zz, zd_out, zd, zs, zr, gram, coef, ra, rb,
    in_sem, t_send, t_recv, d_send, d_recv, v_send, v_recv, h_send, h_recv, b_send, b_recv, r_send, r_recv,
    e_send, e_recv, f_send, f_recv, eb,
):
    s = lax.axis_index("space")
    o = lax.axis_index("orb")
    h, c, q, x = o // 2, o % 2, s // 4, s % 4
    side = (c + q) % 2
    host = (x // 2 + q) % 2
    mine = c == host
    link = 2 * q + side
    has_left, has_right = link > 0, link < 31

    def device(hh, cc, qq, xx):
        return (2 * hh + cc, 4 * qq + xx)

    def along(n):
        n = n % 32
        return device(h, (n + n // 2) % 2, n // 2, x)

    left, right = along(link + 31), along(link + 1)
    up = device(h, c, q, (x + 3) % 4)
    down = device(h, c, q, (x + 1) % 4)
    across = device(1 - h, c, q, x)

    me1 = (x * 2 + h) * 2 + c
    me2 = q

    def peer1(k):
        i = (me1 + k) % 16
        return device((i // 2) % 2, i % 2, q, i // 4)

    def peer2(k):
        return device(h, c, (me2 + k) % 16, x)

    loads = [
        pltpu.make_async_copy(src, dst, in_sem.at[n])
        for n, (src, dst) in enumerate(
            ((x_hbm, x_ref), (type_hbm, type_ref), (table_hbm, table_ref), (step_hbm, step_ref))
        )
    ]
    for cp in loads:
        cp.start()

    barrier = pltpu.get_barrier_semaphore()

    for peer in (peer1, peer2):
        for k in FAR_FIRST:
            pl.semaphore_signal(barrier, inc=1, device_id=peer(k), device_id_type=MESH)

    def rows_of(xx):
        return pl.ds(pl.multiple_of(16 * xx, 16), 16)

    def cols_of(hh):
        return pl.ds(pl.multiple_of(CO * hh, CO), CO)

    def part(ref, xx, hh):
        return ref.at[:, rows_of(xx), cols_of(hh)]

    def remote(src, dst, ss, rs, dev):
        return pltpu.make_async_remote_copy(
            src_ref=src, dst_ref=dst, send_sem=ss, recv_sem=rs, device_id=dev, device_id_type=MESH
        )

    def guarded(cond, fn):
        if cond is None:
            fn()
        else:
            pl.when(cond)(fn)

    half = x % 2

    def scatter(j, k):
        hh, xx = (h + j) % 2, (x + k) % 4
        n = 4 * j + k
        return part(x_hbm, xx, hh), xf.at[o, pl.ds(H + 6 * half, 6), pl.ds(8, 16)], t_send.at[n], t_recv.at[2 * o + half], device(hh, host, q, xx)

    def edges(k):
        return zd_out.at[k], zd.at[c, half], d_send.at[k], d_recv.at[2 * c + half], device(h, host, q, (x + k) % 4)

    def potentials(k, n):
        xx = (x + k) % 4
        return part(vs, xx, h), vf.at[pl.ds(6 * half, 6)], v_send.at[n], v_recv.at[half], device(h, host, q, xx)

    def local_or_remote(a):
        @pl.when(mine)
        def _():
            pltpu.make_async_copy(a[0], a[1], a[3]).start()

        @pl.when(jnp.logical_not(mine))
        def _():
            remote(*a).start()

    pl.semaphore_wait(barrier, 30)

    for k in (2, 1, 3, 0):
        remote(*scatter(1, k)).start()
    for k in (2, 1, 3):
        remote(*scatter(0, k)).start()
    local_or_remote(scatter(0, 0))

    own_ref[...] = table(taps_at(jnp.abs(iota((CO, CO), 0) - iota((CO, CO), 1)), CENTER))
    row, col = iota((16, CO), 0), iota((16, CO), 1)
    target = jnp.where(row < H, CO - H + row, jnp.where(row < 2 * H, row - H, -1))
    pick = jnp.where(col == target, jnp.float32(1.0), jnp.float32(0.0)).astype(jnp.bfloat16)
    pick_ref[...] = jnp.concatenate([pick, pick], axis=1)
    spread_ref[...] = table(taps_at(
        jnp.where(row < H, col + H - row, jnp.where(row < 2 * H, CO + row - H - col, 0)), None
    ))
    gram[...] = jnp.zeros(gram.shape, jnp.float32)
    zr[:, :, :, 2 * H:] = jnp.zeros((4, 2, 3, 16 - 2 * H, CO), jnp.float32)
    for f in (xf, wf, nf, mf):
        @pl.when(jnp.logical_not(has_left))
        def _():
            f[:, 0:H] = jnp.zeros((NORB, H, RW + 16, CO), jnp.float32)

        @pl.when(jnp.logical_not(has_right))
        def _():
            f[:, H + PL:] = jnp.zeros((NORB, H, RW + 16, CO), jnp.float32)

    loads[0].wait()
    for k in range(4):
        edge = x_ref[:, rows_of((x + k) % 4), cols_of(1 - h)].reshape(6 * RW, CO)
        zd_out[k, :, 0:6 * RW] = dot16(pick_ref[...], joined(edge, 1), 1, 1)

    for k in (2, 1, 3):
        remote(*edges(k)).start()
    local_or_remote(edges(0))

    for cp in loads[1:]:
        cp.wait()
    kinds = type_ref[...]
    potential = jnp.zeros(kinds.shape, jnp.float32)
    for kind in range(NTYPES):
        potential = jnp.where(kinds == kind, table_ref[kind], potential)
    vs[...] = potential

    @pl.when(mine)
    def _():
        a = potentials(0, 0)
        pltpu.make_async_copy(a[0], a[1], a[3]).start()
        remote(*potentials(2, 1)).start()

    @pl.when(jnp.logical_not(mine))
    def _():
        remote(*potentials(1, 0)).start()
        remote(*potentials(3, 1)).start()

    A, B = h, 1 - h

    def halo_copies(f, r, pair):
        at = pl.ds(2 * pair, 2)
        m = 10 * r + 5 * pair
        return (
            (has_left, remote(f.at[at, H:2 * H, 8:8 + RW], f.at[at, H + PL:, 8:8 + RW], h_send.at[m], h_recv.at[m + 1], left)),
            (has_right, remote(f.at[at, PL:PL + H, 8:8 + RW], f.at[at, 0:H, 8:8 + RW], h_send.at[m + 1], h_recv.at[m], right)),
            (None, remote(f.at[at, H:H + PL, 8:14], f.at[at, H:H + PL, 24:30], h_send.at[m + 2], h_recv.at[m + 3], up)),
            (None, remote(f.at[at, H:H + PL, 18:24], f.at[at, H:H + PL, 2:8], h_send.at[m + 3], h_recv.at[m + 2], down)),
            (None, remote(zs.at[r, pair, :, 0:2 * H], zr.at[r, pair, :, 0:2 * H], h_send.at[m + 4], h_recv.at[m + 4], across)),
        )

    def share(f, pair):
        return f[pl.ds(2 * pair, 2), H:H + PL, 8:8 + RW].reshape(2 * PL * RW, CO)

    def halo_start(f, r, pair, with_z=True):
        copies = halo_copies(f, r, pair)
        flat = joined(share(f, pair), 1)
        if with_z:
            edge = dot16(pick_ref[...], flat, 1, 1)
            for b in range(3):
                zs[r, pair, b] = edge[:, CO * b:CO * b + CO]
            copies[4][1].start()
        for n in (0, 1, 2, 3):
            guarded(copies[n][0], copies[n][1].start)
        zz[r, pair] = both(dot16(flat, own_ref[...], 1, 0))

    def halo_finish(f, r, pair, with_z=True):
        copies = halo_copies(f, r, pair)
        guarded(has_left, copies[1][1].wait_recv)
        guarded(has_right, copies[0][1].wait_recv)
        copies[2][1].wait_recv()
        copies[3][1].wait_recv()
        if with_z == "late":
            def step(n, carry):
                at = pl.ds(pl.multiple_of(n * RW, RW), RW)
                zz[r, pair, at] = taps_xy(f, r, pair, n // PL, n % PL)
                return carry

            lax.fori_loop(0, 2 * PL, step, 0, unroll=4)
        if with_z:
            copies[4][1].wait_recv()
            zz[r, pair] += both(dot16(joined(jnp.concatenate([zr[r, pair, b] for b in range(3)], axis=1), 0), spread_ref[...], 0, 0))

    def halo_sent(f, r, pair, with_z=True):
        for cond, cp in halo_copies(f, r, pair)[:5 if with_z else 4]:
            guarded(cond, cp.wait_send)

    def kinetic(r, pair, i, p):
        return zz[r, pair, pl.ds(pl.multiple_of((i * PL + p) * RW, RW), RW)]

    def taps_xy(f, r, pair, i, p):
        total = zz[r, pair, pl.ds(pl.multiple_of((i * PL + p) * RW, RW), RW)]
        i = 2 * pair + i
        for n in range(1, H + 1):
            near = f[i, p + H + n, 8:8 + RW] + f[i, p + H - n, 8:8 + RW]
            near = near + f[i, p + H, 8 + n:8 + RW + n] + f[i, p + H, 8 - n:8 + RW - n]
            total = total + SIDE[n - 1] * near
        return total

    def each(fn, pair):
        def step(n, carry):
            fn(pair, n // PL, n % PL)
            return carry
        lax.fori_loop(0, 2 * PL, step, 0, unroll=4)

    def each_plane(fn, init=0):
        return lax.fori_loop(0, PL, fn, init, unroll=2)

    def reduce_start(v, buf, send, recv, me, peer):
        buf[me] = v

        for k in FAR_FIRST:
            remote(buf.at[me], buf.at[me], send, recv, peer(k)).start()

    def reduce_finish(buf, send, recv, peer):
        cp = remote(buf.at[pl.ds(0, 15)], buf.at[pl.ds(0, 15)], send, recv, peer(1))
        cp.wait_send()
        cp.wait_recv()
        return jnp.sum(buf[...], axis=0)

    def local_total():
        v = dot(jnp.ones((8, CO), jnp.float32), gram[...], 1, 1)[0:1]
        return jnp.concatenate([v, jnp.zeros((1, CO - GRAM), jnp.float32)], axis=1)

    def local_sums(rows):
        for n, v in enumerate(rows):
            gram[n:n + 1] = jnp.sum(v, axis=0, keepdims=True)
        return local_total()

    def spread_out(v, n):
        return jnp.broadcast_to(v[:, n:n + 1], (8, CO)) * (1.0 / CELLS)

    def wide(f, i, p):
        return f[i, p + H, 8:8 + RW].reshape(2, 8, CO)

    def narrow(f, i, p):
        return f[i, p].reshape(2, 8, CO)

    def first(pair, i, p):
        k = taps_xy(xf, 0, pair, i, p)
        i = 2 * pair + i
        v = xf[i, p + H, 8:8 + RW]
        wf[i, p + H, 8:8 + RW] = k + vf[p] * v
        nf[i, p + H, 8:8 + RW] = k + SHIFT * v

    def second(pair, i, p):
        k = taps_xy(wf, 1, pair, i, p)
        i = 2 * pair + i
        mf[i, p + H, 8:8 + RW] = k + SHIFT * wf[i, p + H, 8:8 + RW]

    def smooth_x(pair, i, p):
        k = taps_xy(nf, 2, pair, i, p)
        i = 2 * pair + i
        vv[i, p] = P1 * xf[i, p + H, 8:8 + RW] + (P2 + SHIFT * P3) * nf[i, p + H, 8:8 + RW] + P3 * k

    def keep_taps(pair, i, p):
        zz[3, pair, pl.ds(pl.multiple_of((i * PL + p) * RW, RW), RW)] = taps_xy(mf, 3, pair, i, p)

    def arrived(pair):
        for i in range(2):
            for p in range(2):
                ref = xf.at[2 * pair + i, pl.ds(H + 6 * p, 6), pl.ds(8, 16)]
                remote(ref, ref, t_send.at[0], t_recv.at[2 * (2 * pair + i) + p], across).wait_recv()

    arrived(A)
    halo_start(xf, 0, A)
    arrived(B)
    halo_start(xf, 0, B, False)
    for i in range(2):
        for p in range(2):
            remote(zd.at[i, p], zd.at[i, p], d_send.at[0], d_recv.at[2 * i + p], across).wait_recv()
            at = pl.ds((2 * i + p) * 6 * RW, 6 * RW)
            zz[0, A, at] += both(dot16(joined(zd[i, p][:, 0:6 * RW], 0), spread_ref[...], 0, 0))
    for p in range(2):
        remote(vf.at[pl.ds(6 * p, 6)], vf.at[pl.ds(6 * p, 6)], v_send.at[0], v_recv.at[p], across).wait_recv()
    halo_finish(xf, 0, A, False)
    each(first, A)
    halo_start(wf, 1, A)
    halo_start(nf, 2, A)

    def products(pair, with_margin, p, acc):
        xs = [wide(xf, i, p) for i in range(NORB)]
        ws = [wide(wf, 2 * pair + i, p) for i in range(2)]
        terms = [xs[i] * xs[j] for i, j in PAIRS] if with_margin else []
        terms += [xs[j] * w for j in range(NORB) for w in ws]
        return tuple(a + jnp.sum(v, axis=0) for a, v in zip(acc, terms))

    zero = jnp.zeros((8, CO), jnp.float32)
    early = each_plane(functools.partial(products, A, True), (zero,) * 18)
    for n in range(10):
        gram[n:n + 1] = jnp.sum(early[n], axis=0, keepdims=True)
    sums = {}
    halo_finish(xf, 0, B)
    each(first, B)
    halo_start(wf, 1, B)
    acc = each_plane(functools.partial(products, B, False), (zero,) * 8)
    late = acc
    for j in range(NORB):
        for i in range(2):
            a, b = early[10 + 2 * j + i], late[2 * j + i]
            sums[10 + 4 * j + i] = jnp.where(h == 0, a, b)
            sums[12 + 4 * j + i] = jnp.where(h == 0, b, a)
    for n in range(10, 26):
        gram[n:n + 1] = jnp.sum(sums[n], axis=0, keepdims=True)
    reduce_start(local_total(), ra.at[0], r_send.at[0], r_recv.at[0], me1, peer1)
    halo_start(nf, 2, B)

    halo_finish(wf, 1, B)
    each(second, B)
    halo_start(mf, 3, B)
    halo_finish(wf, 1, A)
    each(second, A)
    halo_start(mf, 3, A)
    v = reduce_finish(ra.at[0], r_send.at[0], r_recv.at[0], peer1)
    reduce_start(v, rb.at[0], r_send.at[1], r_recv.at[1], me2, peer2)
    halo_finish(nf, 2, A)
    each(smooth_x, A)
    halo_finish(nf, 2, B)
    each(smooth_x, B)
    halo_finish(mf, 3, A)
    each(keep_taps, A)
    v = reduce_finish(rb.at[0], r_send.at[1], r_recv.at[1], peer2)
    margin = {(i, j): spread_out(v, n) for n, (i, j) in enumerate(PAIRS)}
    low, inv = cholesky(margin)
    for i in range(NORB):
        y = []
        for j in range(NORB):
            t = spread_out(v, 10 + 4 * j + i)
            for k in range(j):
                t = t - low[j, k] * y[k]
            y.append(t * inv[j])
        for j in reversed(range(NORB)):
            t = y[j]
            for k in range(j + 1, NORB):
                t = t - low[k, j] * y[k]
            y[j] = t * inv[j]
            coef[4 * i + j] = step_ref[i] * y[j]

    def prepare(p, carry):
        vs4 = [narrow(vv, j, p) for j in range(NORB)]
        for pair in (A, B):
            for n in range(2):
                i = 2 * pair + n
                t = P1 * wide(wf, i, p) + (P2 + SHIFT * P3) * wide(mf, i, p)
                if pair is A:
                    at = pl.ds(pl.multiple_of((n * PL + p) * RW, RW), RW)
                    t = t + P3 * zz[3, A, at].reshape(2, 8, CO)
                t = wide(xf, i, p) - step_ref[i] * t
                for j in range(NORB):
                    t = t + coef[4 * i + j] * vs4[j]
                base[i, p] = t.reshape(RW, CO)
        return carry

    each_plane(prepare)
    halo_finish(mf, 3, B)

    def move(p, acc):
        for n in range(2):
            i = 2 * B + n
            base[i, p] = base[i, p] - (P3 * step_ref[i]) * taps_xy(mf, 3, B, n, p)
        ms = [narrow(base, i, p) for i in range(NORB)]
        return tuple(a + jnp.sum(ms[i] * ms[j], axis=0) for a, (i, j) in zip(acc, PAIRS))

    acc = each_plane(move, (jnp.zeros((8, CO), jnp.float32),) * 10)
    reduce_start(local_sums(acc), ra.at[1], r_send.at[2], r_recv.at[2], me2, peer2)

    high = h == 1

    def ahead(f, m):
        pp = (x + m) % 2
        return base.at[f, pl.ds(6 * pp, AHEAD)], eb.at[f, :, rows_of(x)], e_send.at[2 * f + m], e_recv.at[4 * f + x], device(1 - h, f % 2, q, 2 * side + pp)

    for f in (0, 1, 2):
        for m in (1, 0):
            guarded(jnp.logical_not(high), remote(*ahead(f, m)).start)
    v = reduce_finish(ra.at[1], r_send.at[2], r_recv.at[2], peer2)
    reduce_start(v, rb.at[1], r_send.at[3], r_recv.at[3], me1, peer1)
    for f in (3,):
        for m in (1, 0):
            guarded(jnp.logical_not(high), remote(*ahead(f, m)).start)
    for f in (0, 1):
        for m in (1, 0):
            guarded(high, remote(*ahead(f, m)).start)
    v = reduce_finish(rb.at[1], r_send.at[3], r_recv.at[3], peer1)
    low, inv = cholesky({(i, j): spread_out(v, n) for n, (i, j) in enumerate(PAIRS)})
    lowinv = {}
    for j in range(NORB):
        lowinv[j, j] = inv[j]
        for i in range(j + 1, NORB):
            t = low[i, j] * lowinv[j, j]
            for k in range(j + 1, i):
                t = t + low[i, k] * lowinv[k, j]
            lowinv[i, j] = -t * inv[i]
    for n, ij in enumerate(PAIRS):
        coef[n] = lowinv[ij]

    def rotate(p):
        ms = [narrow(base, j, p) for j in range(NORB)]
        for i in range(NORB):
            t = None
            for n, (a, j) in enumerate(PAIRS):
                if a == i:
                    term = coef[n] * ms[j]
                    t = term if t is None else t + term
            new[i, p] = t.reshape(RW, CO)

    def back(j, i, m):
        hh, cc, pp = (h + j) % 2, (c + i) % 2, (x + m) % 2
        n = 4 * j + 2 * i + m
        src, dst = new.at[2 * hh + cc, pl.ds(6 * pp + AHEAD * j, 6 - AHEAD * j)], part(out_ref, x, h).at[pl.ds(AHEAD * j, 6 - AHEAD * j)]
        return src, dst, b_send.at[n], b_recv.at[2 * x + h], device(hh, cc, q, 2 * side + pp)

    order = [(j, i, m) for j in (1, 0) for i in (1, 0) for m in (1, 0)]
    for m in (1, 0):
        for p in range(AHEAD, 6):
            rotate(6 * ((x + m) % 2) + p)
        for i in (1, 0):
            remote(*back(1, i, m)).start()
    for p in range(AHEAD):
        rotate(p)
        rotate(6 + p)
    for jim in order[4:]:
        if jim == (0, 0, 0):
            local_or_remote(back(*jim))
        else:
            remote(*back(*jim)).start()

    def came(f):
        for xx in range(4):
            ref = eb.at[f, :, pl.ds(16 * xx, 16)]
            remote(ref, ref, e_send.at[0], e_recv.at[4 * f + xx], across).wait_recv()

    def pass_on(f):
        return remote(eb.at[f], eb.at[f], f_send.at[f], f_recv.at[f], device(h, 1 - c, q, x))

    gives = {0: c == 0, 1: jnp.logical_and(c == 1, high), 2: jnp.logical_and(c == 0, high)}
    takes = {0: c == 1, 1: jnp.logical_and(c == 0, high), 2: jnp.logical_and(c == 1, high)}
    for f in range(NORB):
        @pl.when(jnp.logical_and(c == f % 2, high) if f > 1 else c == f % 2)
        def _():
            came(f)

        if f < 3:
            guarded(gives[f], pass_on(f).start)
    for f in range(3):
        guarded(takes[f], pass_on(f).wait_recv)
    for i in range(NORB):
        @pl.when(o == i)
        def _():
            t = None
            for n, (a, j) in enumerate(PAIRS):
                if a == i:
                    term = coef[n] * eb[j].reshape(8 * AHEAD, 8, CO)
                    t = term if t is None else t + term
            out_ref[0:AHEAD, :, cols_of(1 - h)] = t.reshape(AHEAD, 64, CO)

    unless_mine = jnp.logical_not(mine)
    for k in range(4):
        remote(*scatter(1, k)).wait_send()
        guarded(unless_mine if k == 0 else None, remote(*scatter(0, k)).wait_send)
        guarded(unless_mine if k == 0 else None, remote(*edges(k)).wait_send)

    @pl.when(mine)
    def _():
        remote(*potentials(2, 1)).wait_send()

    @pl.when(unless_mine)
    def _():
        remote(*potentials(1, 0)).wait_send()
        remote(*potentials(3, 1)).wait_send()

    for r, f in enumerate((xf, wf, nf, mf)):
        halo_sent(f, r, A)
        halo_sent(f, r, B, r > 0)
    for jim in order:
        guarded(unless_mine if jim == (0, 0, 0) else None, remote(*back(*jim)).wait_send)
    for f in range(NORB):
        for m in (1, 0):
            guarded(None if f < 2 else jnp.logical_not(high), remote(*ahead(f, m)).wait_send)
    for f in range(3):
        guarded(gives[f], pass_on(f).wait_send)
    for xx in range(4):
        dst = part(out_ref, xx, h)
        remote(dst, dst, b_send.at[0], b_recv.at[2 * xx + h], across).wait_recv()
        dst = part(out_ref, xx, 1 - h).at[pl.ds(AHEAD, 6 - AHEAD)]
        remote(dst, dst, b_send.at[0], b_recv.at[2 * xx + 1 - h], across).wait_recv()


def body(orbitals, atom_type, type_table, step_length):
    shape = orbitals.shape
    slab = shape[1:]
    anywhere = pl.BlockSpec(memory_space=pl.ANY)
    f32 = jnp.float32
    share = (NORB, PL, RW, CO)
    wide = (NORB, PL + 2 * H, RW + 16, CO)
    rows = 2 * PL * RW
    dma = pltpu.SemaphoreType.DMA

    def vmem(*shape):
        return pltpu.VMEM(shape, f32)

    out = pl.pallas_call(
        kernel,
        out_shape=jax.ShapeDtypeStruct(slab, f32),
        in_specs=[anywhere] * 4,
        out_specs=pl.BlockSpec(memory_space=pltpu.VMEM),
        scratch_shapes=[
            vmem(*slab), pltpu.VMEM(slab, jnp.int32), pltpu.SMEM((NTYPES,), f32), pltpu.SMEM((NORB,), f32),
            pltpu.VMEM((2 * CO, 2 * CO), jnp.bfloat16), pltpu.VMEM((16, 2 * CO), jnp.bfloat16), pltpu.VMEM((32, 2 * CO), jnp.bfloat16),
            vmem(*wide), vmem(*wide), vmem(*wide), vmem(*wide),
            vmem(*slab), vmem(PL, RW, CO), vmem(*share), vmem(*share), vmem(*share),
            vmem(4, 2, rows, CO), vmem(4, 16, CO), vmem(2, 2, 16, CO),
            vmem(4, 2, 3, 16, CO), vmem(4, 2, 3, 16, CO),
            vmem(GRAM, CO), vmem(16, 8, CO), vmem(2, 16, 1, CO), vmem(2, 16, 1, CO),
            dma((4,)), dma((8,)), dma((8,)), dma((4,)), dma((4,)), dma((2,)), dma((2,)),
            dma((40,)), dma((40,)), dma((8,)), dma((8,)), dma((4,)), dma((4,)),
            dma((8,)), dma((16,)), dma((3,)), dma((3,)), vmem(NORB, AHEAD, 64, CO),
        ],
        compiler_params=pltpu.CompilerParams(
            collective_id=0, has_side_effects=True, vmem_limit_bytes=55993958
        ),
        name="step",
    )(orbitals.reshape(slab), atom_type, type_table, step_length)
    return out.reshape(shape)


def solution(mesh):
    in_specs = (P("orb", "space", None, None), P("space", None, None), P(), P())
    out_specs = P("orb", "space", None, None)
    return jax.shard_map(body, mesh=mesh, in_specs=in_specs, out_specs=out_specs, check_vma=False)
```

```python
import functools

import jax
import jax.numpy as jnp
from jax import lax
from jax.experimental import pallas as pl
from jax.experimental.pallas import tpu as pltpu
from jax.sharding import PartitionSpec as P

MESH = pl.DeviceIdType.MESH
HIGH = lax.Precision.HIGHEST
CENTER_TAP = -5369.0 / 1800.0
SIDE_TAPS = (12.0 / 7.0, -15.0 / 56.0, 10.0 / 189.0, -1.0 / 112.0, 2.0 / 1925.0, -1.0 / 16632.0)
SHIFT = 1.0
DAMPING = 0.6
DIAGONAL = SHIFT - 1.5 * CENTER_TAP
CELLS = 384 * 64 * 256
NORB = 4
NTYPES = 8

SIDE = tuple(-0.5 * w for w in SIDE_TAPS)
CENTER = -1.5 * CENTER_TAP
W = DAMPING / DIAGONAL
P1, P2, P3 = 3.0 * W, -3.0 * W * W, W * W * W

PL, RW, CO = 12, 16, 128
H = 6
GRAM = 32
AHEAD = 3
FAR_FIRST = (10, 6, 2, 14, 11, 7, 3, 15, 8, 9, 4, 12, 5, 13, 1)
PAIRS = [(i, j) for i in range(NORB) for j in range(i + 1)]


def iota(shape, dim):
    return lax.broadcasted_iota(jnp.int32, shape, dim)


def taps_at(distance, centre):
    out = jnp.zeros(distance.shape, jnp.float32)
    if centre is not None:
        out = jnp.where(distance == 0, jnp.float32(centre), out)
    for n, w in enumerate(SIDE, 1):
        out = jnp.where(distance == n, jnp.float32(w), out)
    return out


def dot(a, b, ca, cb):
    return lax.dot_general(
        a, b, (((ca,), (cb,)), ((), ())), precision=HIGH, preferred_element_type=jnp.float32
    )


def pieces(a):
    high = a.astype(jnp.bfloat16)
    return high, (a - high.astype(jnp.float32)).astype(jnp.bfloat16)


def joined(a, axis):
    return jnp.concatenate(pieces(a), axis=axis)


def dot16(a, b, ca, cb):
    return lax.dot_general(a, b, (((ca,), (cb,)), ((), ())), preferred_element_type=jnp.float32)


def table(a):
    high, low = pieces(a)
    none = jnp.zeros(a.shape, jnp.bfloat16)
    return jnp.concatenate(
        [jnp.concatenate([high, high], axis=0), jnp.concatenate([low, none], axis=0)], axis=1
    )


def both(a):
    return a[:, :CO] + a[:, CO:]


def cholesky(s):
    low = {}
    inv = []
    for i in range(NORB):
        for j in range(i):
            t = s[i, j]
            for k in range(j):
                t = t - low[i, k] * low[j, k]
            low[i, j] = t * inv[j]
        t = s[i, i]
        for k in range(i):
            t = t - low[i, k] * low[i, k]
        root = jnp.sqrt(t)
        low[i, i] = root
        inv.append(1.0 / root)
    return low, inv


def kernel(
    x_hbm, type_hbm, table_hbm, step_hbm, out_ref,
    x_ref, type_ref, table_ref, step_ref, own_ref, pick_ref, spread_ref,
    xf, wf, nf, mf, vs, vf, base, vv, new, zz, zd_out, zd, zs, zr, gram, coef, ra, rb,
    in_sem, t_send, t_recv, d_send, d_recv, v_send, v_recv, h_send, h_recv, b_send, b_recv, r_send, r_recv,
    e_send, e_recv, f_send, f_recv, eb,
):
    s = lax.axis_index("space")
    o = lax.axis_index("orb")
    h, c, q, x = o // 2, o % 2, s // 4, s % 4
    side = (c + q) % 2
    host = (x // 2 + q) % 2
    mine = c == host
    link = 2 * q + side
    has_left, has_right = link > 0, link < 31

    def device(hh, cc, qq, xx):
        return (2 * hh + cc, 4 * qq + xx)

    def along(n):
        n = n % 32
        return device(h, (n + n // 2) % 2, n // 2, x)

    left, right = along(link + 31), along(link + 1)
    up = device(h, c, q, (x + 3) % 4)
    down = device(h, c, q, (x + 1) % 4)
    across = device(1 - h, c, q, x)

    me1 = (x * 2 + h) * 2 + c
    me2 = q

    def peer1(k):
        i = (me1 + k) % 16
        return device((i // 2) % 2, i % 2, q, i // 4)

    def peer2(k):
        return device(h, c, (me2 + k) % 16, x)

    loads = [
        pltpu.make_async_copy(src, dst, in_sem.at[n])
        for n, (src, dst) in enumerate(
            ((x_hbm, x_ref), (type_hbm, type_ref), (table_hbm, table_ref), (step_hbm, step_ref))
        )
    ]
    for cp in loads:
        cp.start()

    barrier = pltpu.get_barrier_semaphore()

    for peer in (peer1, peer2):
        for k in FAR_FIRST:
            pl.semaphore_signal(barrier, inc=1, device_id=peer(k), device_id_type=MESH)

    def rows_of(xx):
        return pl.ds(pl.multiple_of(16 * xx, 16), 16)

    def cols_of(hh):
        return pl.ds(pl.multiple_of(CO * hh, CO), CO)

    def part(ref, xx, hh):
        return ref.at[:, rows_of(xx), cols_of(hh)]

    def remote(src, dst, ss, rs, dev):
        return pltpu.make_async_remote_copy(
            src_ref=src, dst_ref=dst, send_sem=ss, recv_sem=rs, device_id=dev, device_id_type=MESH
        )

    def guarded(cond, fn):
        if cond is None:
            fn()
        else:
            pl.when(cond)(fn)

    half = x % 2

    def scatter(j, k):
        hh, xx = (h + j) % 2, (x + k) % 4
        n = 4 * j + k
        return part(x_hbm, xx, hh), xf.at[o, pl.ds(H + 6 * half, 6), pl.ds(8, 16)], t_send.at[n], t_recv.at[2 * o + half], device(hh, host, q, xx)

    def edges(k):
        return zd_out.at[k], zd.at[c, half], d_send.at[k], d_recv.at[2 * c + half], device(h, host, q, (x + k) % 4)

    def potentials(k, n):
        xx = (x + k) % 4
        return part(vs, xx, h), vf.at[pl.ds(6 * half, 6)], v_send.at[n], v_recv.at[half], device(h, host, q, xx)

    def local_or_remote(a):
        @pl.when(mine)
        def _():
            pltpu.make_async_copy(a[0], a[1], a[3]).start()

        @pl.when(jnp.logical_not(mine))
        def _():
            remote(*a).start()

    pl.semaphore_wait(barrier, 30)

    for k in (2, 1, 3, 0):
        remote(*scatter(1, k)).start()
    for k in (2, 1, 3):
        remote(*scatter(0, k)).start()
    local_or_remote(scatter(0, 0))

    own_ref[...] = table(taps_at(jnp.abs(iota((CO, CO), 0) - iota((CO, CO), 1)), CENTER))
    row, col = iota((16, CO), 0), iota((16, CO), 1)
    target = jnp.where(row < H, CO - H + row, jnp.where(row < 2 * H, row - H, -1))
    pick = jnp.where(col == target, jnp.float32(1.0), jnp.float32(0.0)).astype(jnp.bfloat16)
    pick_ref[...] = jnp.concatenate([pick, pick], axis=1)
    spread_ref[...] = table(taps_at(
        jnp.where(row < H, col + H - row, jnp.where(row < 2 * H, CO + row - H - col, 0)), None
    ))
    gram[...] = jnp.zeros(gram.shape, jnp.float32)
    zr[:, :, :, 2 * H:] = jnp.zeros((4, 2, 3, 16 - 2 * H, CO), jnp.float32)
    for f in (xf, wf, nf, mf):
        @pl.when(jnp.logical_not(has_left))
        def _():
            f[:, 0:H] = jnp.zeros((NORB, H, RW + 16, CO), jnp.float32)

        @pl.when(jnp.logical_not(has_right))
        def _():
            f[:, H + PL:] = jnp.zeros((NORB, H, RW + 16, CO), jnp.float32)

    loads[0].wait()
    for k in range(4):
        edge = x_ref[:, rows_of((x + k) % 4), cols_of(1 - h)].reshape(6 * RW, CO)
        zd_out[k, :, 0:6 * RW] = dot16(pick_ref[...], joined(edge, 1), 1, 1)

    for k in (2, 1, 3):
        remote(*edges(k)).start()
    local_or_remote(edges(0))

    for cp in loads[1:]:
        cp.wait()
    kinds = type_ref[...]
    potential = jnp.zeros(kinds.shape, jnp.float32)
    for kind in range(NTYPES):
        potential = jnp.where(kinds == kind, table_ref[kind], potential)
    vs[...] = potential

    @pl.when(mine)
    def _():
        a = potentials(0, 0)
        pltpu.make_async_copy(a[0], a[1], a[3]).start()
        remote(*potentials(2, 1)).start()

    @pl.when(jnp.logical_not(mine))
    def _():
        remote(*potentials(1, 0)).start()
        remote(*potentials(3, 1)).start()

    A, B = h, 1 - h

    def halo_copies(f, r, pair):
        at = pl.ds(2 * pair, 2)
        m = 10 * r + 5 * pair
        return (
            (has_left, remote(f.at[at, H:2 * H, 8:8 + RW], f.at[at, H + PL:, 8:8 + RW], h_send.at[m], h_recv.at[m + 1], left)),
            (has_right, remote(f.at[at, PL:PL + H, 8:8 + RW], f.at[at, 0:H, 8:8 + RW], h_send.at[m + 1], h_recv.at[m], right)),
            (None, remote(f.at[at, H:H + PL, 8:14], f.at[at, H:H + PL, 24:30], h_send.at[m + 2], h_recv.at[m + 3], up)),
            (None, remote(f.at[at, H:H + PL, 18:24], f.at[at, H:H + PL, 2:8], h_send.at[m + 3], h_recv.at[m + 2], down)),
            (None, remote(zs.at[r, pair, :, 0:2 * H], zr.at[r, pair, :, 0:2 * H], h_send.at[m + 4], h_recv.at[m + 4], across)),
        )

    def share(f, pair):
        return f[pl.ds(2 * pair, 2), H:H + PL, 8:8 + RW].reshape(2 * PL * RW, CO)

    def halo_start(f, r, pair, with_z=True):
        copies = halo_copies(f, r, pair)
        if not with_z:
            for n in (0, 1, 2, 3):
                guarded(copies[n][0], copies[n][1].start)
        flat = joined(share(f, pair), 1)
        if with_z:
            edge = dot16(pick_ref[...], flat, 1, 1)
            for b in range(3):
                zs[r, pair, b] = edge[:, CO * b:CO * b + CO]
            copies[4][1].start()
            for n in (0, 1, 2, 3):
                guarded(copies[n][0], copies[n][1].start)
        zz[r, pair] = both(dot16(flat, own_ref[...], 1, 0))

    def halo_finish(f, r, pair, with_z=True):
        copies = halo_copies(f, r, pair)
        guarded(has_left, copies[1][1].wait_recv)
        guarded(has_right, copies[0][1].wait_recv)
        copies[2][1].wait_recv()
        copies[3][1].wait_recv()
        if with_z == "late":
            def step(n, carry):
                at = pl.ds(pl.multiple_of(n * RW, RW), RW)
                zz[r, pair, at] = taps_xy(f, r, pair, n // PL, n % PL)
                return carry

            lax.fori_loop(0, 2 * PL, step, 0, unroll=4)
        if with_z:
            copies[4][1].wait_recv()
            zz[r, pair] += both(dot16(joined(jnp.concatenate([zr[r, pair, b] for b in range(3)], axis=1), 0), spread_ref[...], 0, 0))

    def halo_sent(f, r, pair, with_z=True):
        for cond, cp in halo_copies(f, r, pair)[:5 if with_z else 4]:
            guarded(cond, cp.wait_send)

    def kinetic(r, pair, i, p):
        return zz[r, pair, pl.ds(pl.multiple_of((i * PL + p) * RW, RW), RW)]

    def taps_xy(f, r, pair, i, p):
        total = zz[r, pair, pl.ds(pl.multiple_of((i * PL + p) * RW, RW), RW)]
        i = 2 * pair + i
        for n in range(1, H + 1):
            near = f[i, p + H + n, 8:8 + RW] + f[i, p + H - n, 8:8 + RW]
            near = near + f[i, p + H, 8 + n:8 + RW + n] + f[i, p + H, 8 - n:8 + RW - n]
            total = total + SIDE[n - 1] * near
        return total

    def each(fn, pair):
        def step(n, carry):
            fn(pair, n // PL, n % PL)
            return carry
        lax.fori_loop(0, 2 * PL, step, 0, unroll=4)

    def each_plane(fn, init=0):
        return lax.fori_loop(0, PL, fn, init, unroll=2)

    def reduce_start(v, buf, send, recv, me, peer):
        buf[me] = v

        for k in FAR_FIRST:
            remote(buf.at[me], buf.at[me], send, recv, peer(k)).start()

    def reduce_finish(buf, send, recv, peer):
        cp = remote(buf.at[pl.ds(0, 15)], buf.at[pl.ds(0, 15)], send, recv, peer(1))
        cp.wait_send()
        cp.wait_recv()
        return jnp.sum(buf[...], axis=0)

    def local_total():
        v = dot(jnp.ones((8, CO), jnp.float32), gram[...], 1, 1)[0:1]
        return jnp.concatenate([v, jnp.zeros((1, CO - GRAM), jnp.float32)], axis=1)

    def local_sums(rows):
        for n, v in enumerate(rows):
            gram[n:n + 1] = jnp.sum(v, axis=0, keepdims=True)
        return local_total()

    def spread_out(v, n):
        return jnp.broadcast_to(v[:, n:n + 1], (8, CO)) * (1.0 / CELLS)

    def wide(f, i, p):
        return f[i, p + H, 8:8 + RW].reshape(2, 8, CO)

    def narrow(f, i, p):
        return f[i, p].reshape(2, 8, CO)

    def first(pair, i, p):
        k = taps_xy(xf, 0, pair, i, p)
        i = 2 * pair + i
        v = xf[i, p + H, 8:8 + RW]
        wf[i, p + H, 8:8 + RW] = k + vf[p] * v
        nf[i, p + H, 8:8 + RW] = k + SHIFT * v

    def second(pair, i, p):
        k = taps_xy(wf, 1, pair, i, p)
        i = 2 * pair + i
        mf[i, p + H, 8:8 + RW] = k + SHIFT * wf[i, p + H, 8:8 + RW]

    def smooth_x(pair, i, p):
        k = taps_xy(nf, 2, pair, i, p)
        i = 2 * pair + i
        vv[i, p] = P1 * xf[i, p + H, 8:8 + RW] + (P2 + SHIFT * P3) * nf[i, p + H, 8:8 + RW] + P3 * k

    def keep_taps(pair, i, p):
        zz[3, pair, pl.ds(pl.multiple_of((i * PL + p) * RW, RW), RW)] = taps_xy(mf, 3, pair, i, p)

    def arrived(pair):
        for i in range(2):
            for p in range(2):
                ref = xf.at[2 * pair + i, pl.ds(H + 6 * p, 6), pl.ds(8, 16)]
                remote(ref, ref, t_send.at[0], t_recv.at[2 * (2 * pair + i) + p], across).wait_recv()

    arrived(A)
    halo_start(xf, 0, A)
    arrived(B)
    halo_start(xf, 0, B, False)
    for i in range(2):
        for p in range(2):
            remote(zd.at[i, p], zd.at[i, p], d_send.at[0], d_recv.at[2 * i + p], across).wait_recv()
            at = pl.ds((2 * i + p) * 6 * RW, 6 * RW)
            zz[0, A, at] += both(dot16(joined(zd[i, p][:, 0:6 * RW], 0), spread_ref[...], 0, 0))
    for p in range(2):
        remote(vf.at[pl.ds(6 * p, 6)], vf.at[pl.ds(6 * p, 6)], v_send.at[0], v_recv.at[p], across).wait_recv()
    halo_finish(xf, 0, A, False)
    each(first, A)
    halo_start(wf, 1, A)
    halo_start(nf, 2, A)

    def products(pair, with_margin, p, acc):
        xs = [wide(xf, i, p) for i in range(NORB)]
        ws = [wide(wf, 2 * pair + i, p) for i in range(2)]
        terms = [xs[i] * xs[j] for i, j in PAIRS] if with_margin else []
        terms += [xs[j] * w for j in range(NORB) for w in ws]
        return tuple(a + jnp.sum(v, axis=0) for a, v in zip(acc, terms))

    zero = jnp.zeros((8, CO), jnp.float32)
    early = each_plane(functools.partial(products, A, True), (zero,) * 18)
    for n in range(10):
        gram[n:n + 1] = jnp.sum(early[n], axis=0, keepdims=True)
    sums = {}
    halo_finish(xf, 0, B)
    each(first, B)
    halo_start(wf, 1, B)
    acc = each_plane(functools.partial(products, B, False), (zero,) * 8)
    late = acc
    for j in range(NORB):
        for i in range(2):
            a, b = early[10 + 2 * j + i], late[2 * j + i]
            sums[10 + 4 * j + i] = jnp.where(h == 0, a, b)
            sums[12 + 4 * j + i] = jnp.where(h == 0, b, a)
    for n in range(10, 26):
        gram[n:n + 1] = jnp.sum(sums[n], axis=0, keepdims=True)
    reduce_start(local_total(), ra.at[0], r_send.at[0], r_recv.at[0], me1, peer1)
    halo_start(nf, 2, B)

    halo_finish(wf, 1, B)
    each(second, B)
    halo_start(mf, 3, B)
    halo_finish(wf, 1, A)
    each(second, A)
    halo_start(mf, 3, A)
    v = reduce_finish(ra.at[0], r_send.at[0], r_recv.at[0], peer1)
    reduce_start(v, rb.at[0], r_send.at[1], r_recv.at[1], me2, peer2)
    halo_finish(nf, 2, A)
    each(smooth_x, A)
    halo_finish(nf, 2, B)
    each(smooth_x, B)
    halo_finish(mf, 3, A)
    each(keep_taps, A)
    v = reduce_finish(rb.at[0], r_send.at[1], r_recv.at[1], peer2)
    margin = {(i, j): spread_out(v, n) for n, (i, j) in enumerate(PAIRS)}
    low, inv = cholesky(margin)
    for i in range(NORB):
        y = []
        for j in range(NORB):
            t = spread_out(v, 10 + 4 * j + i)
            for k in range(j):
                t = t - low[j, k] * y[k]
            y.append(t * inv[j])
        for j in reversed(range(NORB)):
            t = y[j]
            for k in range(j + 1, NORB):
                t = t - low[k, j] * y[k]
            y[j] = t * inv[j]
            coef[4 * i + j] = step_ref[i] * y[j]

    def prepare(p, carry):
        vs4 = [narrow(vv, j, p) for j in range(NORB)]
        for pair in (A, B):
            for n in range(2):
                i = 2 * pair + n
                t = P1 * wide(wf, i, p) + (P2 + SHIFT * P3) * wide(mf, i, p)
                if pair is A:
                    at = pl.ds(pl.multiple_of((n * PL + p) * RW, RW), RW)
                    t = t + P3 * zz[3, A, at].reshape(2, 8, CO)
                t = wide(xf, i, p) - step_ref[i] * t
                for j in range(NORB):
                    t = t + coef[4 * i + j] * vs4[j]
                base[i, p] = t.reshape(RW, CO)
        return carry

    each_plane(prepare)
    halo_finish(mf, 3, B)

    def move(p, acc):
        for n in range(2):
            i = 2 * B + n
            base[i, p] = base[i, p] - (P3 * step_ref[i]) * taps_xy(mf, 3, B, n, p)
        ms = [narrow(base, i, p) for i in range(NORB)]
        return tuple(a + jnp.sum(ms[i] * ms[j], axis=0) for a, (i, j) in zip(acc, PAIRS))

    acc = each_plane(move, (jnp.zeros((8, CO), jnp.float32),) * 10)
    reduce_start(local_sums(acc), ra.at[1], r_send.at[2], r_recv.at[2], me2, peer2)

    high = h == 1

    def ahead(f, m):
        pp = (x + m) % 2
        return base.at[f, pl.ds(6 * pp, AHEAD)], eb.at[f, :, rows_of(x)], e_send.at[2 * f + m], e_recv.at[4 * f + x], device(1 - h, f % 2, q, 2 * side + pp)

    for f in (0, 1, 2):
        for m in (1, 0):
            guarded(jnp.logical_not(high), remote(*ahead(f, m)).start)
    v = reduce_finish(ra.at[1], r_send.at[2], r_recv.at[2], peer2)
    reduce_start(v, rb.at[1], r_send.at[3], r_recv.at[3], me1, peer1)
    for f in (3,):
        for m in (1, 0):
            guarded(jnp.logical_not(high), remote(*ahead(f, m)).start)
    for f in (0, 1):
        for m in (1, 0):
            guarded(high, remote(*ahead(f, m)).start)
    v = reduce_finish(rb.at[1], r_send.at[3], r_recv.at[3], peer1)
    low, inv = cholesky({(i, j): spread_out(v, n) for n, (i, j) in enumerate(PAIRS)})
    lowinv = {}
    for j in range(NORB):
        lowinv[j, j] = inv[j]
        for i in range(j + 1, NORB):
            t = low[i, j] * lowinv[j, j]
            for k in range(j + 1, i):
                t = t + low[i, k] * lowinv[k, j]
            lowinv[i, j] = -t * inv[i]
    for n, ij in enumerate(PAIRS):
        coef[n] = lowinv[ij]

    def rotate(p):
        ms = [narrow(base, j, p) for j in range(NORB)]
        for i in range(NORB):
            t = None
            for n, (a, j) in enumerate(PAIRS):
                if a == i:
                    term = coef[n] * ms[j]
                    t = term if t is None else t + term
            new[i, p] = t.reshape(RW, CO)

    def back(j, i, m):
        hh, cc, pp = (h + j) % 2, (c + i) % 2, (x + m) % 2
        n = 4 * j + 2 * i + m
        src, dst = new.at[2 * hh + cc, pl.ds(6 * pp + AHEAD * j, 6 - AHEAD * j)], part(out_ref, x, h).at[pl.ds(AHEAD * j, 6 - AHEAD * j)]
        return src, dst, b_send.at[n], b_recv.at[2 * x + h], device(hh, cc, q, 2 * side + pp)

    order = [(j, i, m) for j in (1, 0) for i in (1, 0) for m in (1, 0)]
    for m in (1, 0):
        for p in range(AHEAD, 6):
            rotate(6 * ((x + m) % 2) + p)
        for i in (1, 0):
            remote(*back(1, i, m)).start()
    for p in range(AHEAD):
        rotate(p)
        rotate(6 + p)
    for jim in order[4:]:
        if jim == (0, 0, 0):
            local_or_remote(back(*jim))
        else:
            remote(*back(*jim)).start()

    def came(f):
        for xx in range(4):
            ref = eb.at[f, :, pl.ds(16 * xx, 16)]
            remote(ref, ref, e_send.at[0], e_recv.at[4 * f + xx], across).wait_recv()

    def pass_on(f):
        return remote(eb.at[f], eb.at[f], f_send.at[f], f_recv.at[f], device(h, 1 - c, q, x))

    gives = {0: c == 0, 1: jnp.logical_and(c == 1, high), 2: jnp.logical_and(c == 0, high)}
    takes = {0: c == 1, 1: jnp.logical_and(c == 0, high), 2: jnp.logical_and(c == 1, high)}
    for f in range(NORB):
        @pl.when(jnp.logical_and(c == f % 2, high) if f > 1 else c == f % 2)
        def _():
            came(f)

        if f < 3:
            guarded(gives[f], pass_on(f).start)
    for f in range(3):
        guarded(takes[f], pass_on(f).wait_recv)
    for i in range(NORB):
        @pl.when(o == i)
        def _():
            t = None
            for n, (a, j) in enumerate(PAIRS):
                if a == i:
                    term = coef[n] * eb[j].reshape(8 * AHEAD, 8, CO)
                    t = term if t is None else t + term
            out_ref[0:AHEAD, :, cols_of(1 - h)] = t.reshape(AHEAD, 64, CO)

    unless_mine = jnp.logical_not(mine)
    for k in range(4):
        remote(*scatter(1, k)).wait_send()
        guarded(unless_mine if k == 0 else None, remote(*scatter(0, k)).wait_send)
        guarded(unless_mine if k == 0 else None, remote(*edges(k)).wait_send)

    @pl.when(mine)
    def _():
        remote(*potentials(2, 1)).wait_send()

    @pl.when(unless_mine)
    def _():
        remote(*potentials(1, 0)).wait_send()
        remote(*potentials(3, 1)).wait_send()

    for r, f in enumerate((xf, wf, nf, mf)):
        halo_sent(f, r, A)
        halo_sent(f, r, B, r > 0)
    for jim in order:
        guarded(unless_mine if jim == (0, 0, 0) else None, remote(*back(*jim)).wait_send)
    for f in range(NORB):
        for m in (1, 0):
            guarded(None if f < 2 else jnp.logical_not(high), remote(*ahead(f, m)).wait_send)
    for f in range(3):
        guarded(gives[f], pass_on(f).wait_send)
    for xx in range(4):
        dst = part(out_ref, xx, h)
        remote(dst, dst, b_send.at[0], b_recv.at[2 * xx + h], across).wait_recv()
        dst = part(out_ref, xx, 1 - h).at[pl.ds(AHEAD, 6 - AHEAD)]
        remote(dst, dst, b_send.at[0], b_recv.at[2 * xx + 1 - h], across).wait_recv()


def body(orbitals, atom_type, type_table, step_length):
    shape = orbitals.shape
    slab = shape[1:]
    anywhere = pl.BlockSpec(memory_space=pl.ANY)
    f32 = jnp.float32
    share = (NORB, PL, RW, CO)
    wide = (NORB, PL + 2 * H, RW + 16, CO)
    rows = 2 * PL * RW
    dma = pltpu.SemaphoreType.DMA

    def vmem(*shape):
        return pltpu.VMEM(shape, f32)

    out = pl.pallas_call(
        kernel,
        out_shape=jax.ShapeDtypeStruct(slab, f32),
        in_specs=[anywhere] * 4,
        out_specs=pl.BlockSpec(memory_space=pltpu.VMEM),
        scratch_shapes=[
            vmem(*slab), pltpu.VMEM(slab, jnp.int32), pltpu.SMEM((NTYPES,), f32), pltpu.SMEM((NORB,), f32),
            pltpu.VMEM((2 * CO, 2 * CO), jnp.bfloat16), pltpu.VMEM((16, 2 * CO), jnp.bfloat16), pltpu.VMEM((32, 2 * CO), jnp.bfloat16),
            vmem(*wide), vmem(*wide), vmem(*wide), vmem(*wide),
            vmem(*slab), vmem(PL, RW, CO), vmem(*share), vmem(*share), vmem(*share),
            vmem(4, 2, rows, CO), vmem(4, 16, CO), vmem(2, 2, 16, CO),
            vmem(4, 2, 3, 16, CO), vmem(4, 2, 3, 16, CO),
            vmem(GRAM, CO), vmem(16, 8, CO), vmem(2, 16, 1, CO), vmem(2, 16, 1, CO),
            dma((4,)), dma((8,)), dma((8,)), dma((4,)), dma((4,)), dma((2,)), dma((2,)),
            dma((40,)), dma((40,)), dma((8,)), dma((8,)), dma((4,)), dma((4,)),
            dma((8,)), dma((16,)), dma((3,)), dma((3,)), vmem(NORB, AHEAD, 64, CO),
        ],
        compiler_params=pltpu.CompilerParams(
            collective_id=0, has_side_effects=True, vmem_limit_bytes=55993958
        ),
        name="step",
    )(orbitals.reshape(slab), atom_type, type_table, step_length)
    return out.reshape(shape)


def solution(mesh):
    in_specs = (P("orb", "space", None, None), P("space", None, None), P(), P())
    out_specs = P("orb", "space", None, None)
    return jax.shard_map(body, mesh=mesh, in_specs=in_specs, out_specs=out_specs, check_vma=False)
```
